32 devices in a mesh: dp: 4 (over y, core), fsdp: 8 (over z, x).
Axes of the slice: x: 2, y: 2, z: 4, core: 2. Of those that a mesh axis runs over, the one named last changes fastest.
Arguments:
- tokens: bfloat16 [32768, 1024], P(('dp', 'fsdp')), may hold values from -6 to 6
- doc_ids: int32 [32, 1024], P(('dp', 'fsdp')), may hold values from 0 to 7, never falling along the last dimension, each value on 1 to 512 neighbouring positions
- norm_in: bfloat16 [1024], P(('dp', 'fsdp')), may hold values from 0.25 to 1.75
- query_weight: bfloat16 [1024, 1024], P(('dp', 'fsdp')), may hold values from -0.1875 to 0.1875
- latent_weight: bfloat16 [1024, 512], P(('dp', 'fsdp')), may hold values from -0.1875 to 0.1875
- key_up_weight: bfloat16 [512, 512], P(('dp', 'fsdp')), may hold values from -0.375 to 0.375
- value_up_weight: bfloat16 [512, 512], P(('dp', 'fsdp')), may hold values from -0.375 to 0.375
- output_weight: bfloat16 [1024, 1024], P(('dp', 'fsdp')), may hold values from -1.5 to 1.5
- norm_mid: bfloat16 [1024], P(('dp', 'fsdp')), may hold values from 0.25 to 1.75
- gate_weight: bfloat16 [1024, 2816], P(('dp', 'fsdp')), may hold values from -0.1875 to 0.1875
- up_weight: bfloat16 [1024, 2816], P(('dp', 'fsdp')), may hold values from -0.1875 to 0.1875
- down_weight: bfloat16 [2816, 1024], P(('dp', 'fsdp')), may hold values from -0.109375 to 0.109375
- cotangent: bfloat16 [32768, 1024], P(('dp', 'fsdp')), may hold values from -6 to 6
Outputs:
- layer_out: bfloat16 [32768, 1024], P(('dp', 'fsdp'))
- grad_tokens: bfloat16 [32768, 1024], P(('dp', 'fsdp'))
- grad_norm_in: float32 [1024], P(('dp', 'fsdp'))
- grad_query: float32 [1024, 1024], P(('dp', 'fsdp'))
- grad_latent: float32 [1024, 512], P(('dp', 'fsdp'))
- grad_key_up: float32 [512, 512], P(('dp', 'fsdp'))
- grad_value_up: float32 [512, 512], P(('dp', 'fsdp'))
- grad_output: float32 [1024, 1024], P(('dp', 'fsdp'))
- grad_norm_mid: float32 [1024], P(('dp', 'fsdp'))
- grad_gate: float32 [1024, 2816], P(('dp', 'fsdp'))
- grad_up: float32 [1024, 2816], P(('dp', 'fsdp'))
- grad_down: float32 [2816, 1024], P(('dp', 'fsdp'))
The draws below stay inside these ranges and needn't reach their ends.
Inputs may be any that keep to these rules, and one draw needn't show every extreme that they name: `doc_ids`: along each row of 1024 tokens the ids never fall; a document has 1 to 512 tokens of a row.
All inputs are finite; a program needn't handle non-finite values.
Results may differ from the reference program's by a relative error of at most 0.017.
Values may be sent and summed in bfloat16 or wider, within the bound.
No kernel may reach another device: no remote copies, remote signals or barrier semaphores. Data moves between devices by JAX's collectives and lax.ppermute only.
A program may use at most 256 MiB of HBM per device.

```python
import math
import jax
import jax.numpy as jnp
import numpy as np
from jax import lax

D = 1024
H = 16
HD = 64
G = 2
LAT = 256
FF = 2816
HG = 8
SEQ = 1024
DOCS = 8
ROWS = 32
TOKENS = 32768


def steps_of(key, shape, split, low, high):
    factor_of, own = 1.0, jax.random.fold_in(key, 6)
    for axis_at, parts in split:
        heights = jnp.exp(jax.random.uniform(jax.random.fold_in(own, axis_at), (parts,), jnp.float32, low / len(split), high / len(split)))
        factor_of = factor_of * jnp.repeat(heights, shape[axis_at] // parts).reshape([-1 if axis == axis_at else 1 for axis in range(len(shape))])
    return factor_of


def split_up(count, total, reach, slope):
    weights = [(1 << 20) // math.isqrt(grade ** slope) + 1 for grade in range(2, count + 1)]
    spare, holding = total - reach - (count - 1), [1] * (count - 1)
    while spare > 0:
        free = [i for i in range(count - 1) if holding[i] < reach]
        pool, budget = sum([weights[i] for i in free]), spare
        for i in free:
            addition = min(reach - holding[i], max(1, budget * weights[i] // pool), spare)
            holding[i] = holding[i] + addition
            spare = spare - addition
    return np.array([reach] + holding)


def ragged(rng, amount, total, most, skew):
    if amount == 2:
        one = jax.random.randint(rng, (), max(1, total - most), min(most, total - 1) + 1)
        return jnp.stack([one, total - one])
    sizes = jnp.asarray(split_up(amount, total, most, skew), jnp.int32)
    pairs = (amount - 1) // 2
    source_of, sink = sizes[1:1 + 2 * pairs:2], sizes[2:2 + 2 * pairs:2]
    margin = jnp.minimum(source_of - 1, most - sink)
    moved = jax.random.randint(jax.random.fold_in(rng, 1), (pairs,), 0, 1 << 20) % (margin + 1)
    sizes = sizes.at[1:1 + 2 * pairs:2].set(source_of - moved).at[2:2 + 2 * pairs:2].set(sink + moved)
    return sizes[jax.random.permutation(jax.random.fold_in(rng, 2), amount)]


def bell_draw(key, dims, spread, reach, split=(), kind=jnp.bfloat16):
    level = steps_of(key, dims, split, -0.22, 0.18) if split else 1.0
    entries = jax.random.normal(key, dims, jnp.float32) * spread * level
    return jnp.minimum(jnp.maximum(entries, -reach), reach).astype(kind)


def setup_inputs(seed: int = 0) -> dict:
    keys = jax.random.split(jax.random.key(seed), 14)
    return {
        "tokens": bell_draw(keys[0], (TOKENS, D), 1.0, 6.0, ((0, 32),)),
        "doc_ids": jax.vmap(lambda own: jnp.searchsorted(jnp.cumsum(ragged(own, DOCS, SEQ, SEQ // 2, 1)), jnp.arange(SEQ), side="right"))(jax.random.split(keys[1], ROWS)).reshape((ROWS, SEQ)).astype(jnp.int32),
        "norm_in": jnp.clip(1.0 + 0.15 * jax.random.normal(keys[2], (D,), jnp.float32), 0.25, 1.75).astype(jnp.bfloat16),
        "query_weight": bell_draw(keys[3], (D, H * HD), D ** -0.5, 0.1875, ((0, 32),)),
        "latent_weight": bell_draw(keys[4], (D, G * LAT), D ** -0.5, 0.1875, ((0, 32),)),
        "key_up_weight": bell_draw(keys[5], (G * LAT, HG * HD), LAT ** -0.5, 0.375, ((0, 32),)),
        "value_up_weight": bell_draw(keys[6], (G * LAT, HG * HD), LAT ** -0.5, 0.375, ((0, 32),)),
        "output_weight": bell_draw(keys[7], (H * HD, D), (H * HD // 64) ** -0.5, 1.5, ((0, 32),)),
        "norm_mid": jnp.clip(1.0 + 0.15 * jax.random.normal(keys[8], (D,), jnp.float32), 0.25, 1.75).astype(jnp.bfloat16),
        "gate_weight": bell_draw(keys[9], (D, FF), D ** -0.5, 0.1875, ((0, 32),)),
        "up_weight": bell_draw(keys[10], (D, FF), D ** -0.5, 0.1875, ((0, 32),)),
        "down_weight": bell_draw(keys[11], (FF, D), FF ** -0.5, 0.109375, ((0, 32),)),
        "cotangent": bell_draw(keys[12], (TOKENS, D), 1.0, 6.0, ((0, 32),)),
    }


@jax.custom_vjp
def low(v):
    return lax.optimization_barrier(v.astype(jnp.bfloat16)).astype(jnp.float32)

@jax.custom_vjp
def low_back(v):
    return v

def low_keep(v):
    return (low(v), None)

def low_pass(kept, grad):
    return (grad,)

def back_keep(v):
    return (v, None)

def back_low(kept, grad):
    return (low(grad),)
low.defvjp(low_keep, low_pass)
low_back.defvjp(back_keep, back_low)
EPSILON = 1e-05
SCORE_SCALE = 0.125
NEGATIVE = -1e+30
HIGHEST = lax.Precision.HIGHEST

def matmul(left, right):
    return jnp.dot(left, right, precision=HIGHEST)

def rms_scale(values, gain):
    return values * lax.rsqrt(lax.optimization_barrier(jnp.mean(values * values, axis=-1, keepdims=True)) + EPSILON) * gain

def latent_up(latents, weight):
    pieces = [matmul(latents[:, group_index * LAT:(group_index + 1) * LAT], weight[group_index * LAT:(group_index + 1) * LAT]) for group_index in range(G)]
    return jnp.concatenate(pieces, axis=1)

def attend(queries, key_heads, value_heads, doc_row):
    length = queries.shape[0]
    block_rows = min(512, length)
    positions = jnp.arange(length, dtype=jnp.int32)

    def one_block(start_row):
        query_block = lax.dynamic_slice_in_dim(queries, start_row, block_rows, 0)
        doc_block = lax.dynamic_slice_in_dim(doc_row, start_row, block_rows, 0)
        query_pos = start_row + jnp.arange(block_rows, dtype=jnp.int32)
        visible = (doc_block[:, None] == doc_row[None, :]) & (positions[None, :] <= query_pos[:, None])
        scores = low_back(jnp.einsum('qhd,khd->hqk', query_block, key_heads, precision=HIGHEST) * SCORE_SCALE)
        scores = jnp.where(visible[None], scores, NEGATIVE)
        largest = lax.optimization_barrier(jnp.max(scores, axis=-1, keepdims=True))
        powers = jnp.exp(scores - largest)
        weights = low(powers / lax.optimization_barrier(jnp.sum(powers, axis=-1, keepdims=True)))
        return jnp.einsum('hqk,khd->qhd', weights, value_heads, precision=HIGHEST)
    starts = (jnp.arange(length // block_rows, dtype=jnp.int32) * block_rows).astype(jnp.int32)
    return lax.map(jax.checkpoint(one_block), starts).reshape(length, H * HD)

def layer(inputs, doc_row, norm_in, query_weight, latent_weight, key_up_weight, value_up_weight, output_weight, norm_mid, gate_weight, up_weight, down_weight):
    length = inputs.shape[0]
    normed = low(rms_scale(inputs, norm_in))
    queries = low(low_back(matmul(normed, query_weight)))
    latents = low(low_back(matmul(normed, latent_weight)))
    key_heads = low(low_back(latent_up(latents, key_up_weight)))
    value_heads = low(low_back(latent_up(latents, value_up_weight)))
    attended = attend(queries.reshape(length, H, HD), key_heads.reshape(length, H, HD), value_heads.reshape(length, H, HD), doc_row)
    attended = low(low_back(attended))
    hidden = inputs + low_back(matmul(attended, output_weight))
    mid_normed = low(rms_scale(hidden, norm_mid))
    gate_pre = low_back(matmul(mid_normed, gate_weight))
    up_pre = low_back(matmul(mid_normed, up_weight))
    activated = low(low_back(jax.nn.silu(gate_pre) * up_pre))
    return hidden + low_back(matmul(activated, down_weight))

def reference(tokens, doc_ids, norm_in, query_weight, latent_weight, key_up_weight, value_up_weight, output_weight, norm_mid, gate_weight, up_weight, down_weight, cotangent):
    params = tuple((weight.astype(jnp.float32) for weight in (norm_in, query_weight, latent_weight, key_up_weight, value_up_weight, output_weight, norm_mid, gate_weight, up_weight, down_weight)))
    row_count = doc_ids.shape[0]
    inputs = tokens.astype(jnp.float32).reshape(row_count, SEQ, D)
    upstream = cotangent.astype(jnp.float32).reshape(row_count, SEQ, D)

    def one_row(running, row_items):
        input_row, doc_row, cotangent_row = row_items

        def apply_layer(input_value, *weights):
            return layer(input_value, doc_row, *weights)
        output_row, pullback = jax.vjp(apply_layer, input_row, *params)
        gradients = pullback(cotangent_row)
        running = tuple((summed + gradient for summed, gradient in zip(running, gradients[1:])))
        return (running, (output_row.astype(jnp.bfloat16), gradients[0].astype(jnp.bfloat16)))
    zero_sums = tuple((jnp.zeros(param.shape, jnp.float32) for param in params))
    totals, (outputs, input_grads) = lax.scan(one_row, zero_sums, (inputs, doc_ids, upstream))
    return (outputs.reshape(TOKENS, D), input_grads.reshape(TOKENS, D), totals[0], totals[1], totals[2], totals[3], totals[4], totals[5], totals[6], totals[7], totals[8], totals[9])
```

```python
import functools

import jax
import jax.numpy as jnp
from jax import lax
from jax.experimental import pallas as pl
from jax.experimental.pallas import tpu as pltpu
from jax.sharding import PartitionSpec as P

HD = 64
G = 2
HG = 8
PAIR = 128
EPSILON = 1e-05
SCORE_SCALE = 0.125
NEGATIVE = -1e30
LOG2E = 1.4426950408889634
F32 = jnp.float32
BF16 = jnp.bfloat16
TILE = 256
VMEM_LIMIT = 60 * 1024 * 1024


def nn(a, b):
    return lax.dot_general(a, b, (((1,), (0,)), ((), ())), preferred_element_type=F32)


def nt(a, b):
    return lax.dot_general(a, b, (((1,), (1,)), ((), ())), preferred_element_type=F32)


def tn(a, b):
    return lax.dot_general(a, b, (((0,), (0,)), ((), ())), preferred_element_type=F32)


def params(**extra):
    return pltpu.CompilerParams(vmem_limit_bytes=VMEM_LIMIT, **extra)


def whole(shape):
    return pl.BlockSpec(shape, lambda *_: (0,) * len(shape))


def rows_of(tile, width):
    return pl.BlockSpec((tile, width), lambda i: (i, 0))


def shape_of(shape, dtype):
    return jax.ShapeDtypeStruct(shape, dtype)


def project_kernel(
    tok_ref, wq_ref, wl_ref, wg_ref, ku_ref, vu_ref, q_ref, lat_ref, k_ref, v_ref, n_ref, gain_ref
):
    @pl.when(pl.program_id(0) == 0)
    def _():
        gain_ref[...] = wg_ref[...].astype(F32).T[0:8, :]

    x = tok_ref[...].astype(F32)
    root = lax.rsqrt(jnp.mean(x * x, axis=-1, keepdims=True) + EPSILON)
    normed = (x * root * gain_ref[0:1, :]).astype(BF16)
    n_ref[...] = normed
    q_ref[...] = (nn(normed, wq_ref[...]).astype(BF16).astype(F32) * SCORE_SCALE).astype(BF16)
    lat = nn(normed, wl_ref[...]).astype(BF16)
    lat_ref[...] = lat
    wide = lat.shape[1] // G
    out = k_ref.shape[1] // G
    for g in range(G):
        piece = lat[:, g * wide : (g + 1) * wide]
        k_ref[:, g * out : (g + 1) * out] = nn(
            piece, ku_ref[g * wide : (g + 1) * wide, :]
        ).astype(BF16)
        v_ref[:, g * out : (g + 1) * out] = nn(
            piece, vu_ref[g * wide : (g + 1) * wide, :]
        ).astype(BF16)


def project(tokens, first, ku, vu):
    count, d = tokens.shape
    latw = ku.shape[0]
    width = G * ku.shape[1]
    return pl.pallas_call(
        project_kernel,
        grid=(count // TILE,),
        in_specs=[
            rows_of(TILE, d),
            pl.BlockSpec((d, width), lambda i: (0, 0)),
            pl.BlockSpec((d, latw), lambda i: (0, width // latw)),
            pl.BlockSpec((d, PAIR), lambda i: (0, (width + 2 * latw) // PAIR)),
            whole(ku.shape),
            whole(vu.shape),
        ],
        out_specs=[
            rows_of(TILE, width),
            rows_of(TILE, latw),
            rows_of(TILE, width),
            rows_of(TILE, width),
            rows_of(TILE, d),
            whole((8, d)),
        ],
        out_shape=[
            shape_of((count, width), BF16),
            shape_of((count, latw), BF16),
            shape_of((count, width), BF16),
            shape_of((count, width), BF16),
            shape_of((count, d), BF16),
            shape_of((8, d), F32),
        ],
        compiler_params=params(),
        name="project",
    )(tokens, first, first, first, ku, vu)


def window_of(doc_ref, block):
    start = block * TILE
    here = doc_ref[start]
    one = (doc_ref[start - 1] == here).astype(jnp.int32) if block >= 1 else 0
    two = (doc_ref[start - TILE - 1] == here).astype(jnp.int32) if block >= 2 else 0
    return one + two


def attend_kernel(doc_ref, q_ref, k_ref, v_ref, col_ref, row_ref, o_ref, lse_ref, bias_ref):
    length = q_ref.shape[0]
    blocks = length // TILE
    lane = lax.broadcasted_iota(jnp.int32, (TILE, PAIR), 1)
    low = lane < HD

    @pl.when(pl.program_id(0) == 0)
    def _():
        for b in range(blocks):
            first = max(0, b - 2)
            width = (b - first + 1) * TILE
            qpos = b * TILE + lax.broadcasted_iota(jnp.int32, (TILE, width), 0)
            kpos = first * TILE + lax.broadcasted_iota(jnp.int32, (TILE, width), 1)
            same = (
                col_ref[b * TILE : (b + 1) * TILE, 0:1]
                == row_ref[0:1, first * TILE : first * TILE + width]
            )
            bias_ref[b, :, 3 * TILE - width :] = jnp.where(
                same & (kpos <= qpos), 0.0, NEGATIVE
            )

    for b in range(blocks):
        q = q_ref[b * TILE : (b + 1) * TILE, :]
        zero = jnp.zeros_like(q)
        heads = (jnp.where(low, q, zero), jnp.where(low, zero, q))
        seen = window_of(doc_ref, b)

        def run(extra, b=b, heads=heads):
            width = (extra + 1) * TILE
            at = (b - extra) * TILE
            k = k_ref[at : at + width, :]
            v = v_ref[at : at + width, :]
            vlow = lax.broadcasted_iota(jnp.int32, v.shape, 1) < HD
            one = jnp.ones_like(v)
            values = (jnp.where(vlow, v, one), jnp.where(vlow, one, v))
            bias = bias_ref[b, :, 3 * TILE - width :]
            outs = []
            sums = []
            for h in range(2):
                s = nt(heads[h], k) * LOG2E + bias
                top = jnp.max(s, axis=-1, keepdims=True)
                p = jnp.exp2(s - top)
                o = nn(p.astype(BF16), values[h])
                total = pltpu.roll(o, HD, 1)
                outs.append(o / total)
                sums.append(top + jnp.log2(total))
            o_ref[b * TILE : (b + 1) * TILE, :] = jnp.where(low, outs[0], outs[1]).astype(BF16)
            both = jnp.where(low, sums[0], sums[1]).T
            lse_ref[0, 0:1, b * TILE : (b + 1) * TILE] = both[0:1, :]
            lse_ref[0, 1:2, b * TILE : (b + 1) * TILE] = both[HD : HD + 1, :]

        for extra in range(min(b, 2) + 1):
            pl.when(seen == extra)(functools.partial(run, extra))


def attend(doc, q, k, v):
    length, width = q.shape
    pairs = width // PAIR
    col = doc.reshape(length, 1)
    row = doc.reshape(1, length)
    return pl.pallas_call(
        attend_kernel,
        grid_spec=pltpu.PrefetchScalarGridSpec(
            num_scalar_prefetch=1,
            grid=(pairs,),
            in_specs=[
                pl.BlockSpec((length, PAIR), lambda i, *_: (0, i)),
                pl.BlockSpec((length, PAIR), lambda i, *_: (0, i)),
                pl.BlockSpec((length, PAIR), lambda i, *_: (0, i)),
                whole((length, 1)),
                whole((1, length)),
            ],
            out_specs=[
                pl.BlockSpec((length, PAIR), lambda i, *_: (0, i)),
                pl.BlockSpec((1, 8, length), lambda i, *_: (i, 0, 0)),
            ],
            scratch_shapes=[pltpu.VMEM((length // TILE, TILE, 3 * TILE), F32)],
        ),
        out_shape=[shape_of((length, width), BF16), shape_of((pairs, 8, length), F32)],
        compiler_params=params(),
        name="attend",
    )(doc.reshape(length), q, k, v, col, row)


def attend_back_kernel(
    doc_ref,
    q_ref,
    k_ref,
    v_ref,
    o_ref,
    do_ref,
    lse_ref,
    col_ref,
    row_ref,
    dq_ref,
    dk_ref,
    dv_ref,
    bias_ref,
    dk_acc,
    dv_acc,
):
    length = q_ref.shape[0]
    blocks = length // TILE
    lane = lax.broadcasted_iota(jnp.int32, (TILE, PAIR), 1)
    low = lane < HD

    @pl.when(pl.program_id(0) == 0)
    def _():
        for b in range(blocks):
            first = max(0, b - 2)
            width = (b - first + 1) * TILE
            kpos = first * TILE + lax.broadcasted_iota(jnp.int32, (width, TILE), 0)
            qpos = b * TILE + lax.broadcasted_iota(jnp.int32, (width, TILE), 1)
            same = (
                col_ref[first * TILE : first * TILE + width, 0:1]
                == row_ref[0:1, b * TILE : (b + 1) * TILE]
            )
            bias_ref[b, 3 * TILE - width :, :] = jnp.where(
                same & (kpos <= qpos), 0.0, NEGATIVE
            )

    dk_acc[...] = jnp.zeros_like(dk_acc)
    dv_acc[...] = jnp.zeros_like(dv_acc)
    for b in range(blocks):
        rows = slice(b * TILE, (b + 1) * TILE)
        q = q_ref[rows, :]
        do = do_ref[rows, :]
        zero = jnp.zeros_like(q)
        prod = (do.astype(F32) * o_ref[rows, :].astype(F32)).T
        inner = (
            jnp.sum(prod[0:HD, :], axis=0, keepdims=True),
            jnp.sum(prod[HD:, :], axis=0, keepdims=True),
        )
        seen = window_of(doc_ref, b)

        def run(extra, b=b, rows=rows, q=q, do=do, zero=zero, inner=inner):
            width = (extra + 1) * TILE
            at = (b - extra) * TILE
            keys = slice(at, at + width)
            k = k_ref[keys, :]
            v = v_ref[keys, :]
            bias = bias_ref[b, 3 * TILE - width :, :]
            parts = []
            dks = []
            dvs = []
            for h in range(2):
                mine = low if h == 0 else ~low
                qh = jnp.where(mine, q, zero)
                doh = jnp.where(mine, do, zero)
                s = nt(k, qh) * LOG2E + bias
                p = jnp.exp2(s - lse_ref[0, h : h + 1, rows])
                dp = nt(v, doh)
                ds = (p * (dp - inner[h])).astype(BF16)
                dvs.append(nn(p.astype(BF16), doh))
                dks.append(nn(ds, qh))
                parts.append(tn(ds, k))
            dv_acc[keys, :] += dvs[0] + dvs[1]
            dk_acc[keys, :] += dks[0] + dks[1]
            dq_ref[rows, :] = (jnp.where(low, parts[0], parts[1]) * SCORE_SCALE).astype(BF16)

        for extra in range(min(b, 2) + 1):
            pl.when(seen == extra)(functools.partial(run, extra))
    dk_ref[...] = dk_acc[...].astype(BF16)
    dv_ref[...] = dv_acc[...].astype(BF16)


def attend_back(doc, q, k, v, o, do, lse):
    length, width = q.shape
    pairs = width // PAIR
    col = doc.reshape(length, 1)
    row = doc.reshape(1, length)
    strip = pl.BlockSpec((length, PAIR), lambda i, *_: (0, i))
    return pl.pallas_call(
        attend_back_kernel,
        grid_spec=pltpu.PrefetchScalarGridSpec(
            num_scalar_prefetch=1,
            grid=(pairs,),
            in_specs=[strip] * 5
            + [
                pl.BlockSpec((1, 8, length), lambda i, *_: (i, 0, 0)),
                whole((length, 1)),
                whole((1, length)),
            ],
            out_specs=[strip] * 3,
            scratch_shapes=[
                pltpu.VMEM((length // TILE, 3 * TILE, TILE), F32),
                pltpu.VMEM((length, PAIR), F32),
                pltpu.VMEM((length, PAIR), F32),
            ],
        ),
        out_shape=[shape_of((length, width), BF16)] * 3,
        compiler_params=params(),
        name="attend_back",
    )(doc.reshape(length), q, k, v, o, do, lse, col, row)


def middle_kernel(att_ref, wo_ref, tok_ref, gain_ref, hid_ref, mid_ref, midt_ref):
    hid = tok_ref[...].astype(F32) + nn(att_ref[...], wo_ref[...])
    hid_ref[...] = hid
    root = lax.rsqrt(jnp.mean(hid * hid, axis=-1, keepdims=True) + EPSILON)
    mid = (hid * root * gain_ref[1:2, :]).astype(BF16)
    mid_ref[...] = mid
    midt_ref[...] = mid.T


def middle(att, wo, tokens, gains):
    count, d = tokens.shape
    width = att.shape[1]
    return pl.pallas_call(
        middle_kernel,
        grid=(count // TILE,),
        in_specs=[rows_of(TILE, width), wo[1], rows_of(TILE, d), whole((8, d))],
        out_specs=[
            rows_of(TILE, d),
            rows_of(TILE, d),
            pl.BlockSpec((d, TILE), lambda i: (0, i)),
        ],
        out_shape=[
            shape_of((count, d), F32),
            shape_of((count, d), BF16),
            shape_of((d, count), BF16),
        ],
        compiler_params=params(),
        name="middle",
    )(att, wo[0], tokens, gains)


def feed_kernel(
    mid_ref,
    midt_ref,
    cot_ref,
    hid_ref,
    gmid_in_ref,
    gate_ref,
    up_ref,
    down_ref,
    out_ref,
    gmid_ref,
    ggate_ref,
    gup_ref,
    gdown_ref,
    act_s,
    ggp_s,
    gup_s,
):
    count = mid_ref.shape[0]

    @pl.when(pl.program_id(0) == 0)
    def _():
        out_ref[...] = hid_ref[...]
        if gmid_in_ref is None:
            gmid_ref[...] = jnp.zeros_like(gmid_ref)
        else:
            gmid_ref[...] = gmid_in_ref[...]

    gate = gate_ref[...]
    up = up_ref[...]
    down = down_ref[...]

    @pl.loop(0, count // TILE)
    def _(t):
        rows = pl.ds(pl.multiple_of(t * TILE, TILE), TILE)
        m = mid_ref[rows, :]
        gate_pre = nn(m, gate)
        up_pre = nn(m, up)
        grad_act = nt(cot_ref[rows, :], down).astype(BF16).astype(F32)
        sig = 1.0 / (1.0 + jnp.exp(-gate_pre))
        silu = gate_pre * sig
        act = (silu * up_pre).astype(BF16)
        ggp = (grad_act * up_pre * (sig * (1.0 + gate_pre * (1.0 - sig)))).astype(BF16)
        gup = (grad_act * silu).astype(BF16)
        act_s[rows, :] = act
        ggp_s[rows, :] = ggp
        gup_s[rows, :] = gup
        out_ref[rows, :] += nn(act, down)
        gmid_ref[rows, :] += nt(ggp, gate) + nt(gup, up)

    ggp = ggp_s[...]
    gup = gup_s[...]

    @pl.loop(0, midt_ref.shape[0] // TILE)
    def _(t):
        rows = pl.ds(pl.multiple_of(t * TILE, TILE), TILE)
        m = midt_ref[rows, :]
        ggate_ref[rows, :] = nn(m, ggp).astype(BF16)
        gup_ref[rows, :] = nn(m, gup).astype(BF16)

    gdown_ref[...] = tn(act_s[...], cot_ref[...]).astype(BF16)


def feed(mid, midt, cot, hid, gmid, gate, up, down, steps):
    count, d = mid.shape
    args = [mid, midt, cot, hid]
    specs = [whole((count, d)), whole((d, count)), whole((count, d)), whole((count, d))]
    if gmid is None:
        body = lambda a, b, c, e, *rest: feed_kernel(a, b, c, e, None, *rest)
    else:
        body = feed_kernel
        args.append(gmid)
        specs.append(whole((count, d)))
    wide = steps * TILE
    return pl.pallas_call(
        body,
        grid=(steps,),
        in_specs=specs + [gate[1], up[1], down[1]],
        out_specs=[
            whole((count, d)),
            whole((count, d)),
            pl.BlockSpec((d, TILE), lambda i: (0, i)),
            pl.BlockSpec((d, TILE), lambda i: (0, i)),
            pl.BlockSpec((TILE, d), lambda i: (i, 0)),
        ],
        out_shape=[
            shape_of((count, d), F32),
            shape_of((count, d), F32),
            shape_of((d, wide), BF16),
            shape_of((d, wide), BF16),
            shape_of((wide, d), BF16),
        ],
        scratch_shapes=[pltpu.VMEM((count, TILE), BF16)] * 3,
        compiler_params=params(),
        name="feed",
    )(*args, gate[0], up[0], down[0])


def middle_back_kernel(
    gmid_ref, hid_ref, cot_ref, att_ref, wo_ref, gain_ref, ghid_ref, gatt_ref, go_ref, gn_ref, acc
):
    step = pl.program_id(0)

    @pl.when(step == 0)
    def _():
        acc[...] = jnp.zeros_like(acc)
        gn_ref[...] = jnp.zeros_like(gn_ref)

    hid = hid_ref[...]
    root = lax.rsqrt(jnp.mean(hid * hid, axis=-1, keepdims=True) + EPSILON)
    unit = hid * root
    gmid = gmid_ref[...]
    gn_ref[0:1, :] += jnp.sum(gmid * unit, axis=0, keepdims=True)
    t = gmid * gain_ref[1:2, :]
    inner = jnp.mean(t * unit, axis=-1, keepdims=True)
    ghid = cot_ref[...].astype(F32) + root * (t - unit * inner)
    ghid_ref[...] = ghid
    branch = ghid.astype(BF16)
    gatt_ref[...] = nt(branch, wo_ref[...]).astype(BF16)
    acc[...] += tn(att_ref[...], branch)

    @pl.when(step == pl.num_programs(0) - 1)
    def _():
        go_ref[...] = acc[...].astype(BF16)


def middle_back(gmid, hid, cot, att, wo, gains):
    count, d = hid.shape
    width = att.shape[1]
    return pl.pallas_call(
        middle_back_kernel,
        grid=(count // TILE,),
        in_specs=[
            rows_of(TILE, d),
            rows_of(TILE, d),
            rows_of(TILE, d),
            rows_of(TILE, width),
            wo[1],
            whole((8, d)),
        ],
        out_specs=[rows_of(TILE, d), rows_of(TILE, width), whole((width, d)), whole((8, d))],
        out_shape=[
            shape_of((count, d), F32),
            shape_of((count, width), BF16),
            shape_of((width, d), BF16),
            shape_of((8, d), F32),
        ],
        scratch_shapes=[pltpu.VMEM((width, d), F32)],
        compiler_params=params(),
        name="middle_back",
    )(gmid, hid, cot, att, wo[0], gains)


def project_back_kernel(
    gq_ref,
    gk_ref,
    gv_ref,
    lat_ref,
    n_ref,
    tok_ref,
    ghid_ref,
    wq_ref,
    wl_ref,
    ku_ref,
    vu_ref,
    gain_ref,
    gtok_ref,
    gwq_ref,
    gwl_ref,
    gku_ref,
    gvu_ref,
    gn_ref,
    acc_q,
    acc_l,
    acc_k,
    acc_v,
):
    step = pl.program_id(0)

    @pl.when(step == 0)
    def _():
        for ref in (acc_q, acc_l, acc_k, acc_v, gn_ref):
            ref[...] = jnp.zeros_like(ref)

    wide = ku_ref.shape[0] // G
    out = ku_ref.shape[1]
    lat = lat_ref[...]
    pieces = []
    for g in range(G):
        gk = gk_ref[:, g * out : (g + 1) * out]
        gv = gv_ref[:, g * out : (g + 1) * out]
        own = slice(g * wide, (g + 1) * wide)
        pieces.append(nt(gk, ku_ref[own, :]) + nt(gv, vu_ref[own, :]))
        acc_k[own, :] += tn(lat[:, own], gk)
        acc_v[own, :] += tn(lat[:, own], gv)
    glat = jnp.concatenate(pieces, axis=1).astype(BF16)
    gq = gq_ref[...]
    acc_q[...] += tn(n_ref[...], gq)
    acc_l[...] += tn(n_ref[...], glat)
    gin = nt(gq, wq_ref[...]) + nt(glat, wl_ref[...])
    x = tok_ref[...].astype(F32)
    root = lax.rsqrt(jnp.mean(x * x, axis=-1, keepdims=True) + EPSILON)
    unit = x * root
    gn_ref[0:1, :] += jnp.sum(gin * unit, axis=0, keepdims=True)
    t = gin * gain_ref[0:1, :]
    inner = jnp.mean(t * unit, axis=-1, keepdims=True)
    gtok_ref[...] = (ghid_ref[...] + root * (t - unit * inner)).astype(BF16)

    @pl.when(step == pl.num_programs(0) - 1)
    def _():
        gwq_ref[...] = acc_q[...].astype(BF16)
        gwl_ref[...] = acc_l[...].astype(BF16)
        gku_ref[...] = acc_k[...].astype(BF16)
        gvu_ref[...] = acc_v[...].astype(BF16)


def project_back(gq, gk, gv, lat, normed, tokens, ghid, first, ku, vu, gains):
    count, d = tokens.shape
    width = gq.shape[1]
    latw = lat.shape[1]
    return pl.pallas_call(
        project_back_kernel,
        grid=(count // TILE,),
        in_specs=[
            rows_of(TILE, width),
            rows_of(TILE, width),
            rows_of(TILE, width),
            rows_of(TILE, latw),
            rows_of(TILE, d),
            rows_of(TILE, d),
            rows_of(TILE, d),
            pl.BlockSpec((d, width), lambda i: (0, 0)),
            pl.BlockSpec((d, latw), lambda i: (0, width // latw)),
            whole(ku.shape),
            whole(vu.shape),
            whole((8, d)),
        ],
        out_specs=[
            rows_of(TILE, d),
            whole((d, width)),
            whole((d, latw)),
            whole(ku.shape),
            whole(vu.shape),
            whole((8, d)),
        ],
        out_shape=[
            shape_of((count, d), BF16),
            shape_of((d, width), BF16),
            shape_of((d, latw), BF16),
            shape_of(ku.shape, BF16),
            shape_of(vu.shape, BF16),
            shape_of((8, d), F32),
        ],
        scratch_shapes=[
            pltpu.VMEM((d, width), F32),
            pltpu.VMEM((d, latw), F32),
            pltpu.VMEM(ku.shape, F32),
            pltpu.VMEM(vu.shape, F32),
        ],
        compiler_params=params(),
        name="project_back",
    )(gq, gk, gv, lat, normed, tokens, ghid, first, first, ku, vu, gains)


def swap(values, axis_name, bit):
    size = lax.axis_size(axis_name)
    return lax.ppermute(values, axis_name, [(i, i ^ bit) for i in range(size)])


def bits_of(axis_name):
    size = lax.axis_size(axis_name)
    return [1 << i for i in range(size.bit_length() - 1)]


def owner_dims(values):
    names = [("dp", bit) for bit in reversed(bits_of("dp"))]
    names += [("fsdp", bit) for bit in reversed(bits_of("fsdp"))]
    rows = values.shape[0] >> len(names)
    return values.reshape((2,) * len(names) + (rows, values.shape[1])), names


def halve(values, names, which):
    at = names.index(which)
    axis_name, bit = which
    mine = (lax.axis_index(axis_name) // bit) % 2
    keep = lax.dynamic_index_in_dim(values, mine, at, keepdims=False)
    send = lax.dynamic_index_in_dim(values, 1 - mine, at, keepdims=False)
    came = swap(send, axis_name, bit)
    rest = names[:at] + names[at + 1 :]
    return (keep.astype(F32) + came.astype(F32)).astype(BF16), rest


def scatter_sum(values):
    split, names = owner_dims(values)
    split, names = halve(split, names, ("dp", 1))
    outer = [("dp", bit) for bit in bits_of("dp")[1:]]
    inner = [("fsdp", bit) for bit in bits_of("fsdp")]
    orders = (inner[:1] + outer + inner[1:], outer + inner)
    columns = values.shape[1]
    cut = columns // 256 * 128
    done = []
    for order, part in zip(orders, (split[..., :cut], split[..., cut:])):
        left = names
        for which in order:
            part, left = halve(part, left, which)
        done.append(part)
    return jnp.concatenate(done, axis=-1)


def shards(
    tokens,
    doc_ids,
    norm_in,
    query_weight,
    latent_weight,
    key_up_weight,
    value_up_weight,
    output_weight,
    norm_mid,
    gate_weight,
    up_weight,
    down_weight,
    cotangent,
):
    both = ("dp", "fsdp")
    devices = lax.axis_size("dp") * lax.axis_size("fsdp")
    own_rows, d = query_weight.shape
    d_all = own_rows * devices
    latw = latent_weight.shape[1]
    up_rows, up_width = key_up_weight.shape
    ff = gate_weight.shape[1]
    length = doc_ids.shape[1]

    gains = jnp.stack([norm_in, norm_mid], axis=1)
    gains = jnp.pad(gains, ((0, 0), (0, PAIR - 2)))
    packed = jnp.concatenate(
        [
            query_weight,
            latent_weight,
            jnp.concatenate([key_up_weight, value_up_weight], axis=0),
            gains,
        ],
        axis=1,
    )
    first = lax.all_gather(packed, both, axis=0, tiled=True)
    second = lax.all_gather(
        jnp.concatenate([output_weight, gate_weight, up_weight], axis=1), both, axis=0, tiled=True
    )
    down = lax.all_gather(down_weight, both, axis=0, tiled=True)

    ups = first[:, d + latw : d + latw + up_width].reshape(devices, 2, up_rows, up_width)
    ku = ups[:, 0].reshape(devices * up_rows, up_width)
    vu = ups[:, 1].reshape(devices * up_rows, up_width)

    q, lat, k, v, normed, gain_rows = project(tokens, first, ku, vu)
    att, lse = attend(doc_ids, q, k, v)
    wo = (second, pl.BlockSpec((d_all, d), lambda i: (0, 0)))
    hid, mid, midt = middle(att, wo, tokens, gain_rows)

    gate_at = d // TILE
    up_at = (d + ff) // TILE
    steps = ff // TILE
    out, gmid, ggate, gup, gdown = feed(
        mid,
        midt,
        cotangent,
        hid,
        None,
        (second, pl.BlockSpec((d_all, TILE), lambda i: (0, gate_at + i))),
        (second, pl.BlockSpec((d_all, TILE), lambda i: (0, up_at + i))),
        (down, pl.BlockSpec((TILE, d), lambda i: (i, 0))),
        steps,
    )
    layer_out = out.astype(BF16)
    ghid, gatt, go, gnorm_mid = middle_back(gmid, hid, cotangent, att, wo, gain_rows)
    gq, gk, gv = attend_back(doc_ids, q, k, v, att, gatt, lse)
    gtok, gwq, gwl, gku, gvu, gnorm_in = project_back(
        gq, gk, gv, lat, normed, tokens, ghid, first, ku, vu, gain_rows
    )
    s_gu = scatter_sum(jnp.concatenate([ggate, gup], axis=1))
    s_down = scatter_sum(gdown)
    s_o = scatter_sum(go)
    gnorms = jnp.stack([gnorm_in[0], gnorm_mid[0]], axis=1).astype(BF16)
    gups = jnp.concatenate(
        [gku.reshape(devices, up_rows, up_width), gvu.reshape(devices, up_rows, up_width)], axis=1
    ).reshape(d_all, up_width)
    s_first = scatter_sum(
        jnp.concatenate([gwq, gwl, gups, jnp.pad(gnorms, ((0, 0), (0, PAIR - 2)))], axis=1)
    )
    s_first = s_first.astype(F32)
    at = d + latw
    return (
        layer_out,
        gtok,
        s_first[:, at + up_width],
        s_first[:, :d],
        s_first[:, d:at],
        s_first[:up_rows, at : at + up_width],
        s_first[up_rows:, at : at + up_width],
        s_o.astype(F32),
        s_first[:, at + up_width + 1],
        s_gu[:, :ff].astype(F32),
        s_gu[:, ff:].astype(F32),
        s_down.astype(F32),
    )


def solution(mesh):
    split = ("dp", "fsdp")
    flat, matrix = P(split), P(split, None)
    return jax.shard_map(
        shards,
        mesh=mesh,
        in_specs=(
            matrix,
            matrix,
            flat,
            matrix,
            matrix,
            matrix,
            matrix,
            matrix,
            flat,
            matrix,
            matrix,
            matrix,
            matrix,
        ),
        out_specs=(
            matrix,
            matrix,
            flat,
            matrix,
            matrix,
            matrix,
            matrix,
            matrix,
            flat,
            matrix,
            matrix,
            matrix,
        ),
        check_vma=False,
    )
```

```python
import functools

import jax
import jax.numpy as jnp
from jax import lax
from jax.experimental import pallas as pl
from jax.experimental.pallas import tpu as pltpu
from jax.sharding import PartitionSpec as P

HD = 64
G = 2
HG = 8
PAIR = 128
EPSILON = 1e-05
SCORE_SCALE = 0.125
NEGATIVE = -1e30
LOG2E = 1.4426950408889634
F32 = jnp.float32
BF16 = jnp.bfloat16
TILE = 256
QT = 128
SPAN = 4
PP = 2
PPB = 2
VMEM_LIMIT = 60 * 1024 * 1024


def nn(a, b):
    return lax.dot_general(a, b, (((1,), (0,)), ((), ())), preferred_element_type=F32)


def nt(a, b):
    return lax.dot_general(a, b, (((1,), (1,)), ((), ())), preferred_element_type=F32)


def tn(a, b):
    return lax.dot_general(a, b, (((0,), (0,)), ((), ())), preferred_element_type=F32)


def params(**extra):
    return pltpu.CompilerParams(vmem_limit_bytes=VMEM_LIMIT, **extra)


def whole(shape):
    return pl.BlockSpec(shape, lambda *_: (0,) * len(shape))


def rows_of(tile, width):
    return pl.BlockSpec((tile, width), lambda i: (i, 0))


def cost(micros):
    return pl.CostEstimate(flops=int(micros * 1.1e9), bytes_accessed=0, transcendentals=0)


def shape_of(shape, dtype):
    return jax.ShapeDtypeStruct(shape, dtype)


def project_kernel(
    tok_ref,
    wq_ref,
    wl_ref,
    wg_ref,
    ku_ref,
    vu_ref,
    q_ref,
    lat_ref,
    latt_ref,
    k_ref,
    v_ref,
    nt_ref,
    gain_ref,
):
    @pl.when(pl.program_id(0) == 0)
    def _():
        gain_ref[...] = wg_ref[...].astype(F32).T[0:8, :]

    x = tok_ref[...].astype(F32)
    root = lax.rsqrt(jnp.mean(x * x, axis=-1, keepdims=True) + EPSILON)
    normed = (x * root * gain_ref[0:1, :]).astype(BF16)
    nt_ref[...] = normed.T
    lat = nn(normed, wl_ref[...]).astype(BF16)
    lat_ref[...] = lat
    latt_ref[...] = lat.T
    q_ref[...] = (nn(normed, wq_ref[...]).astype(BF16).astype(F32) * SCORE_SCALE).astype(BF16)
    wide = lat.shape[1] // G
    out = k_ref.shape[1] // G
    for g in range(G):
        piece = lat[:, g * wide : (g + 1) * wide]
        k_ref[:, g * out : (g + 1) * out] = nn(
            piece, ku_ref[g * wide : (g + 1) * wide, :]
        ).astype(BF16)
        v_ref[:, g * out : (g + 1) * out] = nn(
            piece, vu_ref[g * wide : (g + 1) * wide, :]
        ).astype(BF16)


def columns_of(height, tile):
    return pl.BlockSpec((height, tile), lambda i: (0, i))


def project(tokens, first, ku, vu):
    count, d = tokens.shape
    latw = ku.shape[0]
    width = G * ku.shape[1]
    return pl.pallas_call(
        project_kernel,
        grid=(count // TILE,),
        in_specs=[
            rows_of(TILE, d),
            pl.BlockSpec((d, width), lambda i: (0, 0)),
            pl.BlockSpec((d, latw), lambda i: (0, (width + d) // latw)),
            pl.BlockSpec((d, PAIR), lambda i: (0, (width + d + 2 * latw) // PAIR)),
            whole(ku.shape),
            whole(vu.shape),
        ],
        out_specs=[
            rows_of(TILE, width),
            rows_of(TILE, latw),
            columns_of(latw, TILE),
            rows_of(TILE, width),
            rows_of(TILE, width),
            columns_of(d, TILE),
            whole((8, d)),
        ],
        out_shape=[
            shape_of((count, width), BF16),
            shape_of((count, latw), BF16),
            shape_of((latw, count), BF16),
            shape_of((count, width), BF16),
            shape_of((count, width), BF16),
            shape_of((d, count), BF16),
            shape_of((8, d), F32),
        ],
        cost_estimate=cost(10),
        compiler_params=params(),
        name="project",
    )(tokens, first, first, first, ku, vu)


def visible(doc):
    length = doc.shape[1]
    ids = doc.reshape(length)
    blocks = []
    padded = jnp.concatenate([jnp.full((SPAN * QT,), -1, ids.dtype), ids])
    for b in range(length // QT):
        keys = jnp.arange((b - SPAN) * QT, (b + 1) * QT)
        own = ids[b * QT : (b + 1) * QT]
        theirs = padded[b * QT : (b + SPAN + 1) * QT]
        queries = jnp.arange(b * QT, (b + 1) * QT)
        seen = (theirs[:, None] == own[None, :]) & (keys[:, None] <= queries[None, :])
        blocks.append(jnp.where(seen, 0.0, NEGATIVE))
    return jnp.stack(blocks).astype(BF16)


def split_heads(values):
    low = lax.broadcasted_iota(jnp.int32, values.shape, 1) < HD
    zero = jnp.zeros_like(values)
    return jnp.concatenate([jnp.where(low, values, zero), jnp.where(low, zero, values)], axis=0)


def attend_kernel(q_ref, k_ref, v_ref, mask_ref, o_ref, ot_ref, lse_ref):
    length = q_ref.shape[0]
    low = lax.broadcasted_iota(jnp.int32, (QT, PAIR), 1) < HD
    for b in range(length // QT):
        rows = slice(b * QT, (b + 1) * QT)
        extra = min(b, SPAN)
        keys = slice((b - extra) * QT, (b + 1) * QT)
        bias = mask_ref[b, (SPAN - extra) * QT :, :].astype(F32)
        bias = jnp.concatenate([bias, bias], axis=1)
        for pair in range(PP):
            cols = slice(pair * PAIR, (pair + 1) * PAIR)
            s = nt(k_ref[keys, cols], split_heads(q_ref[rows, cols])) * LOG2E + bias
            top = jnp.max(s, axis=0, keepdims=True)
            p = jnp.exp2(s - top).astype(BF16)
            v = v_ref[keys, cols]
            r = tn(p, jnp.concatenate([v, jnp.ones_like(v)], axis=1))
            r = jnp.where(
                jnp.concatenate([low, low], axis=1), r[:QT], r[QT:]
            )
            o = r[:, :PAIR] / r[:, PAIR:]
            o_ref[rows, cols] = o.astype(BF16)
            ot_ref[cols, rows] = o.T.astype(BF16)
            total = jnp.log2(r[:, PAIR:].T)
            lse_ref[pair, 0:1, rows] = top[:, :QT] + total[0:1]
            lse_ref[pair, 1:2, rows] = top[:, QT:] + total[HD : HD + 1]


def attend(mask, q, k, v, start, pairs):
    length = q.shape[0]
    width = pairs * PAIR
    wide = PP * PAIR
    strip = pl.BlockSpec((length, wide), lambda i: (0, start // PP + i))
    return pl.pallas_call(
        attend_kernel,
        grid_spec=pltpu.PrefetchScalarGridSpec(
            num_scalar_prefetch=0,
            grid=(pairs // PP,),
            in_specs=[strip, strip, strip, whole(mask.shape)],
            out_specs=[
                pl.BlockSpec((length, wide), lambda i: (0, i)),
                pl.BlockSpec((wide, length), lambda i: (i, 0)),
                pl.BlockSpec((PP, 8, length), lambda i: (i, 0, 0)),
            ],
        ),
        out_shape=[
            shape_of((length, width), BF16),
            shape_of((width, length), BF16),
            shape_of((pairs, 8, length), F32),
        ],
        cost_estimate=cost(2.5 * pairs),
        compiler_params=params(),
        name="attend",
    )(q, k, v, mask)


def attend_back_kernel(
    q_ref,
    k_ref,
    v_ref,
    o_ref,
    do_ref,
    lse_ref,
    mask_ref,
    dq_ref,
    dk_ref,
    dv_ref,
    dk_acc,
    dv_acc,
):
    length = q_ref.shape[0]
    low = lax.broadcasted_iota(jnp.int32, (QT, PAIR), 1) < HD
    dk_acc[...] = jnp.zeros_like(dk_acc)
    dv_acc[...] = jnp.zeros_like(dv_acc)
    kts = [k_ref[:, pair * PAIR : (pair + 1) * PAIR].T for pair in range(PPB)]
    for b in range(length // QT):
        rows = slice(b * QT, (b + 1) * QT)
        extra = min(b, SPAN)
        keys = slice((b - extra) * QT, (b + 1) * QT)
        bias = mask_ref[b, (SPAN - extra) * QT :, :].astype(F32)
        bias = jnp.concatenate([bias, bias], axis=1)
        for pair in range(PPB):
            cols = slice(pair * PAIR, (pair + 1) * PAIR)
            do = do_ref[rows, cols]
            prod = (do.astype(F32) * o_ref[rows, cols].astype(F32)).T
            inner = jnp.concatenate(
                [
                    jnp.sum(prod[:HD], axis=0, keepdims=True),
                    jnp.sum(prod[HD:], axis=0, keepdims=True),
                ],
                axis=1,
            )
            lse = jnp.concatenate(
                [lse_ref[pair, 0:1, rows], lse_ref[pair, 1:2, rows]], axis=1
            )
            qs = split_heads(q_ref[rows, cols])
            dos = split_heads(do)
            k = k_ref[keys, cols]
            p = jnp.exp2(nt(k, qs) * LOG2E + bias - lse)
            ds = (p * (nt(v_ref[keys, cols], dos) - inner)).astype(BF16)
            dv_acc[keys, cols] += nn(p.astype(BF16), dos)
            dk_acc[keys, cols] += nn(ds, qs)
            dq = nn(kts[pair][:, keys], ds) * SCORE_SCALE
            dq = jnp.concatenate([dq[:HD, :QT], dq[HD:, QT:]], axis=0)
            dq_ref[rows, cols] = dq.T.astype(BF16)
    dk_ref[...] = dk_acc[...].astype(BF16)
    dv_ref[...] = dv_acc[...].astype(BF16)


def attend_back(mask, q, k, v, o, do, lse, start, at, pairs):
    length = q.shape[0]
    width = pairs * PAIR
    wide = PPB * PAIR
    strip = pl.BlockSpec((length, wide), lambda i: (0, start // PPB + i))
    own = pl.BlockSpec((length, wide), lambda i: (0, i))
    return pl.pallas_call(
        attend_back_kernel,
        grid_spec=pltpu.PrefetchScalarGridSpec(
            num_scalar_prefetch=0,
            grid=(pairs // PPB,),
            in_specs=[
                strip,
                strip,
                strip,
                pl.BlockSpec((length, wide), lambda i: (0, at // PPB + i)),
                strip,
                pl.BlockSpec((PPB, 8, length), lambda i: (at // PPB + i, 0, 0)),
                whole(mask.shape),
            ],
            out_specs=[own] * 3,
            scratch_shapes=[
                pltpu.VMEM((length, wide), F32),
                pltpu.VMEM((length, wide), F32),
            ],
        ),
        out_shape=[shape_of((length, width), BF16)] * 3,
        cost_estimate=cost(3.5 * pairs),
        compiler_params=params(),
        name="attend_back",
    )(q, k, v, o, do, lse, mask)


def middle_kernel(*refs):
    att_refs = refs[:-6]
    wo_ref, tok_ref, gain_ref, hid_ref, mid_ref, midt_ref = refs[-6:]
    att = jnp.concatenate([ref[...] for ref in att_refs], axis=1)
    hid = tok_ref[...].astype(F32) + nn(att, wo_ref[...])
    hid_ref[...] = hid
    root = lax.rsqrt(jnp.mean(hid * hid, axis=-1, keepdims=True) + EPSILON)
    mid = (hid * root * gain_ref[1:2, :]).astype(BF16)
    mid_ref[...] = mid
    midt_ref[...] = mid.T


def middle(att, wo, tokens, gains):
    count, d = tokens.shape
    return pl.pallas_call(
        middle_kernel,
        grid=(count // TILE,),
        in_specs=[rows_of(TILE, x.shape[1]) for x in att]
        + [wo[1], rows_of(TILE, d), whole((8, d))],
        out_specs=[rows_of(TILE, d), rows_of(TILE, d), columns_of(d, TILE)],
        out_shape=[
            shape_of((count, d), F32),
            shape_of((count, d), BF16),
            shape_of((d, count), BF16),
        ],
        cost_estimate=cost(8),
        compiler_params=params(),
        name="middle",
    )(*att, wo[0], tokens, gains)


def unfold_kernel(own_rows, down_rows, in_ref, out_ref):
    d = out_ref.shape[1]
    for device in range(in_ref.shape[0] // own_rows):
        for fold in range(in_ref.shape[1] // d):
            count = min(own_rows, down_rows - fold * own_rows)
            at = device * down_rows + fold * own_rows
            out_ref[at : at + count, :] = in_ref[
                device * own_rows : device * own_rows + count, fold * d : (fold + 1) * d
            ]


def unfold(wide, own_rows, down_rows, d):
    folds = -(-down_rows // own_rows)
    devices = wide.shape[0] // own_rows
    if own_rows % 16 or devices % 8:
        down = wide[:, : folds * d].reshape(devices, own_rows, folds, d).transpose(0, 2, 1, 3)
        down = down.reshape(devices, folds * own_rows, d)[:, :down_rows]
        return down.reshape(devices * down_rows, d)
    return pl.pallas_call(
        functools.partial(unfold_kernel, own_rows, down_rows),
        grid=(devices // 8,),
        in_specs=[pl.BlockSpec((8 * own_rows, folds * d), lambda i: (i, 0))],
        out_specs=pl.BlockSpec((8 * down_rows, d), lambda i: (i, 0)),
        out_shape=shape_of((devices * down_rows, d), BF16),
        cost_estimate=cost(5),
        compiler_params=params(),
        name="unfold",
    )(wide)


def owner_rows(core_ref, pair, height, mine, span=None):
    core = core_ref[0]
    first = 2 * pair if span is None else 2 * pair % span
    which = first + (core if mine else 1 - core)
    return pl.ds(pl.multiple_of(which * height, height), height)


def feed_kernel(first, last, core_ref, *refs):
    refs = list(refs)
    mid_ref, midt_ref, cot_ref, from_ref = refs[:4]
    del refs[:4]
    gfrom_ref = None
    if not first:
        gfrom_ref = refs[0]
        del refs[:2]
    gate_ref, up_ref, down_ref, out_ref, gmid_ref, keep_ref, send_ref, gdown_ref = refs[:8]
    out_acc, gmid_acc, act_s, ggp_s, gup_s = refs[8:]
    count = mid_ref.shape[0]

    @pl.when(pl.program_id(0) == 0)
    def _():
        out_acc[...] = from_ref[...]
        if first:
            gmid_acc[...] = jnp.zeros_like(gmid_acc)
        else:
            gmid_acc[...] = gfrom_ref[...]

    gate = gate_ref[...]
    up = up_ref[...]
    down = down_ref[...]
    step = 1024

    @pl.loop(0, count // step)
    def _(t):
        rows = pl.ds(pl.multiple_of(t * step, step), step)
        m = mid_ref[rows, :]
        gate_pre = nn(m, gate)
        up_pre = nn(m, up)
        grad_act = nt(cot_ref[rows, :], down)
        sig = 0.5 * jnp.tanh(0.5 * gate_pre) + 0.5
        silu = gate_pre * sig
        act = (silu * up_pre).astype(BF16)
        ggp = (grad_act * up_pre * (sig + silu * (1.0 - sig))).astype(BF16)
        gup = (grad_act * silu).astype(BF16)
        act_s[rows, :] = act
        ggp_s[rows, :] = ggp
        gup_s[rows, :] = gup
        out_acc[rows, :] += nn(act, down)
        gmid_acc[rows, :] += nt(ggp, gate) + nt(gup, up)

    ggp = ggp_s[...]
    gup = gup_s[...]
    _, pairs, height, _ = keep_ref.shape

    for mine, ref in ((False, send_ref), (True, keep_ref)):
        m = jnp.concatenate([midt_ref[owner_rows(core_ref, p, height, mine), :] for p in range(pairs)], axis=0)
        ref[0] = nn(m, ggp).astype(BF16).reshape(ref.shape[1:])
        ref[1] = nn(m, gup).astype(BF16).reshape(ref.shape[1:])

    gdown = tn(act_s[...], cot_ref[...]).astype(BF16)
    half = gdown.shape[1] // 2
    gdown_ref[0] = gdown[:, :half]
    gdown_ref[1] = gdown[:, half:]

    @pl.when(pl.program_id(0) == pl.num_programs(0) - 1)
    def _():
        out_ref[...] = out_acc[...].astype(out_ref.dtype)
        gmid_ref[...] = gmid_acc[...]


def feed(core, mid, midt, cot, start, before, gate, up, down, span, lead, n_dp, ff):
    count, d = mid.shape
    first, last = before is None, span[1] * TILE == ff
    at, steps = span[0], span[1] - span[0]
    args = [mid, midt, cot, start]
    specs = [whole((count, d)), whole((d, count)), whole((count, d)), whole((count, d))]
    alias = {}
    if not first:
        args += list(before)
        specs += [whole((count, d)), pl.BlockSpec(memory_space=pl.ANY)]
        alias = {6: 4}
    height = d // n_dp
    strip = pl.BlockSpec((2, n_dp // 2, height, TILE), lambda i, *_: (0, 0, 0, i + lead // TILE))
    grads = shape_of((2, n_dp // 2, height, lead + steps * TILE), BF16)
    return pl.pallas_call(
        functools.partial(feed_kernel, first, last),
        grid_spec=pltpu.PrefetchScalarGridSpec(
            num_scalar_prefetch=1,
            grid=(steps,),
            in_specs=specs
            + [
                pl.BlockSpec((d, TILE), lambda i, *_: (0, gate[1] + at + i)),
                pl.BlockSpec((d, TILE), lambda i, *_: (0, up[1] + at + i)),
                pl.BlockSpec((TILE, d), lambda i, *_: (at + i, 0)),
            ],
            out_specs=[
                whole((count, d)),
                whole((count, d)),
                strip,
                strip,
                pl.BlockSpec((2, TILE, d // 2), lambda i, *_: (0, at + i, 0)),
            ],
            scratch_shapes=[pltpu.VMEM((count, d), F32)] * 2
            + [pltpu.VMEM((count, TILE), BF16)] * 3,
        ),
        out_shape=[
            shape_of((count, d), BF16 if last else F32),
            shape_of((count, d), F32),
            grads,
            grads,
            shape_of((2, ff, d // 2), BF16),
        ],
        input_output_aliases=alias,
        cost_estimate=cost(7.5 * steps),
        compiler_params=params(),
        name="feed",
    )(core, *args, gate[0], up[0], down)


def middle_back_kernel(
    core_ref,
    gmid_ref,
    hid_ref,
    cot_ref,
    *refs,
):
    attt_refs = refs[:-10]
    (
        wo_ref,
        gain_ref,
        keep_in,
        send_in,
        ghid_ref,
        gatt_ref,
        keep_ref,
        send_ref,
        gn_ref,
        branch_s,
    ) = refs[-10:]
    step = pl.program_id(0)
    tile = hid_ref.shape[0]

    @pl.when(step == 0)
    def _():
        gn_ref[...] = jnp.zeros_like(gn_ref)

    hid = hid_ref[...]
    root = lax.rsqrt(jnp.mean(hid * hid, axis=-1, keepdims=True) + EPSILON)
    unit = hid * root
    gmid = gmid_ref[...]
    gn_ref[0:1, :] += jnp.sum(gmid * unit, axis=0, keepdims=True)
    t = gmid * gain_ref[1:2, :]
    inner = jnp.mean(t * unit, axis=-1, keepdims=True)
    ghid = cot_ref[...].astype(F32) + root * (t - unit * inner)
    ghid_ref[...] = ghid
    branch = ghid.astype(BF16)
    gatt_ref[...] = nt(branch, wo_ref[...]).astype(BF16)
    branch_s[pl.ds(pl.multiple_of(step * tile, tile), tile), :] = branch

    @pl.when(step == pl.num_programs(0) - 1)
    def _():
        half = branch_s.shape[1] // 2
        _, pairs, height, _ = keep_ref.shape
        tall = attt_refs[0].shape[0]
        for p in range(pairs):
            for mine, ref in ((False, send_ref), (True, keep_ref)):
                attt_ref = attt_refs[2 * p * height // tall]
                rows = attt_ref[owner_rows(core_ref, p, height, mine, tall // height), :]
                grad = nn(rows, branch_s[...]).astype(BF16)
                ref[0, p] = grad[:, :half]
                ref[1, p] = grad[:, half:]


def middle_back(core, gmid, hid, cot, attt, wo, gains, keep, send):
    count, d = hid.shape
    width = sum(x.shape[0] for x in attt)
    pairs, height = keep.shape[1:3]
    anywhere = pl.BlockSpec(memory_space=pl.ANY)
    strip = pl.BlockSpec((2, pairs, height, d // 2), lambda i, *_: (0, 0, 0, 0))
    tile = lambda wide: pl.BlockSpec((TILE, wide), lambda i, *_: (i, 0))
    return pl.pallas_call(
        middle_back_kernel,
        grid_spec=pltpu.PrefetchScalarGridSpec(
            num_scalar_prefetch=1,
            grid=(count // TILE,),
            in_specs=[
                tile(d),
                tile(d),
                tile(d),
            ]
            + [whole(x.shape) for x in attt]
            + [
                wo[1],
                whole((8, d)),
                anywhere,
                anywhere,
            ],
            out_specs=[tile(d), tile(width), strip, strip, whole((8, d))],
            scratch_shapes=[pltpu.VMEM((count, d), BF16)],
        ),
        out_shape=[
            shape_of((count, d), F32),
            shape_of((count, width), BF16),
            shape_of(keep.shape, BF16),
            shape_of(send.shape, BF16),
            shape_of((8, d), F32),
        ],
        input_output_aliases={6 + len(attt): 2, 7 + len(attt): 3},
        cost_estimate=cost(12),
        compiler_params=params(),
        name="middle_back",
    )(core, gmid, hid, cot, *attt, wo[0], gains, keep, send)


def interleave(up_rows, height):
    to = lax.broadcasted_iota(jnp.int32, (height, height), 0)
    start = lax.broadcasted_iota(jnp.int32, (height, height), 1)
    turn, row = to // (2 * up_rows), to % (2 * up_rows)
    late = (row >= up_rows).astype(jnp.int32)
    want = turn * up_rows + row - late * up_rows + late * (height // 2)
    return (start == want).astype(F32).astype(BF16)


def project_back_kernel(
    up_rows,
    core_ref,
    *refs,
):
    parts = (len(refs) - 17) // 3
    gq_refs, gk_refs, gv_refs = refs[:parts], refs[parts : 2 * parts], refs[2 * parts : 3 * parts]
    (
        latt_ref,
        nt_ref,
        tok_ref,
        ghid_ref,
        wq_ref,
        wl_ref,
        ku_ref,
        vu_ref,
        gain_ref,
        gn_mid_ref,
        gtok_ref,
        keep_ref,
        send_ref,
        glat_s,
        gn_s,
        gku_s,
        gvu_s,
    ) = refs[3 * parts :]
    step = pl.program_id(0)
    tile = tok_ref.shape[0]
    rows = pl.ds(pl.multiple_of(step * tile, tile), tile)

    @pl.when(step == 0)
    def _():
        gn_s[...] = jnp.zeros_like(gn_s)

    wide = ku_ref.shape[0] // G
    out = ku_ref.shape[1]
    each = parts // G
    strip = out // each
    pieces = []
    gin = jnp.zeros(tok_ref.shape, F32)
    for g in range(G):
        own = slice(g * wide, (g + 1) * wide)
        glat = jnp.zeros((tile, wide), F32)
        for j in range(each):
            part = g * each + j
            cols = slice(j * strip, (j + 1) * strip)
            glat += nt(gk_refs[part][rows, :], ku_ref[own, cols])
            glat += nt(gv_refs[part][rows, :], vu_ref[own, cols])
            gin += nt(gq_refs[part][rows, :], wq_ref[:, part * strip : (part + 1) * strip])
        pieces.append(glat)
    glat = jnp.concatenate(pieces, axis=1).astype(BF16)
    glat_s[rows, :] = glat
    gin += nt(glat, wl_ref[...])
    x = tok_ref[...].astype(F32)
    root = lax.rsqrt(jnp.mean(x * x, axis=-1, keepdims=True) + EPSILON)
    unit = x * root
    gn_s[0:1, :] += jnp.sum(gin * unit, axis=0, keepdims=True)
    t = gin * gain_ref[0:1, :]
    inner = jnp.mean(t * unit, axis=-1, keepdims=True)
    gtok_ref[...] = (ghid_ref[...] + root * (t - unit * inner)).astype(BF16)

    @pl.when(step == pl.num_programs(0) - 1)
    def _():
        _, pairs, height, _ = keep_ref.shape
        width = parts * strip
        latw = glat_s.shape[1]
        for g in range(G):
            own = slice(g * wide, (g + 1) * wide)
            for j in range(each):
                cols = slice(j * strip, (j + 1) * strip)
                gku_s[own, cols] = nn(latt_ref[own, :], gk_refs[g * each + j][...])
                gvu_s[own, cols] = nn(latt_ref[own, :], gv_refs[g * each + j][...])
        d = gn_s.shape[1]
        norm_in = jnp.broadcast_to(gn_s[0:1, :], (PAIR, d)).astype(BF16)
        norm_mid = jnp.broadcast_to(gn_mid_ref[0:1, :], (PAIR, d)).astype(BF16)
        gn_cols = (norm_in.T, norm_mid.T)
        own_rows = 2 * up_rows
        owners = height // own_rows
        core = core_ref[0]
        for p in range(pairs):
            for mine, ref in ((False, send_ref), (True, keep_ref)):
                which = 2 * p + (core if mine else 1 - core)
                at = pl.ds(pl.multiple_of(which * height, height), height)
                m = nt_ref[at, :]
                for part in range(parts):
                    cols = slice(part * strip, (part + 1) * strip)
                    ref[0, p, :, cols] = nn(m, gq_refs[part][...]).astype(BF16)
                ref[1, p, :, 0:latw] = nn(m, glat_s[...]).astype(BF16)
                near = pl.ds(pl.multiple_of(which * (height // 2), height // 2), height // 2)
                keys, values = gku_s[near, :], gvu_s[near, :]
                if up_rows % 8:
                    ups = nn(interleave(up_rows, height), jnp.concatenate([keys, values], axis=0).astype(BF16))
                else:
                    pieces = []
                    for j in range(owners):
                        pieces.append(keys[j * up_rows : (j + 1) * up_rows])
                        pieces.append(values[j * up_rows : (j + 1) * up_rows])
                    ups = jnp.concatenate(pieces, axis=0)
                ref[1, p, :, latw : latw + out] = ups.astype(BF16)
                for h in range(2):
                    a, b = (gn_cols[h][(2 * p + c) * height :][:height] for c in range(2))
                    flip = (core == 0) if mine else (core == 1)
                    ref[h, p, :, width:] = jnp.where(flip, a, b)


def project_back(core, gq, gk, gv, latt, nt_, tokens, ghid, first, ku, vu, gains, gn_mid, n_dp, up_rows):
    count, d = tokens.shape
    parts = len(gq)
    width = sum(x.shape[1] for x in gq)
    latw = latt.shape[0]
    height = d // n_dp
    tile = lambda wide: pl.BlockSpec((TILE, wide), lambda i, *_: (i, 0))
    grads = (2, n_dp // 2, height, width + PAIR)
    return pl.pallas_call(
        functools.partial(project_back_kernel, up_rows),
        grid_spec=pltpu.PrefetchScalarGridSpec(
            num_scalar_prefetch=1,
            grid=(count // TILE,),
            in_specs=[whole(x.shape) for x in (*gq, *gk, *gv)]
            + [
                whole((latw, count)),
                whole((d, count)),
                tile(d),
                tile(d),
                pl.BlockSpec((d, width), lambda i, *_: (0, 0)),
                pl.BlockSpec((d, latw), lambda i, *_: (0, (width + d) // latw)),
                whole(ku.shape),
                whole(vu.shape),
                whole((8, d)),
                whole((8, d)),
            ],
            out_specs=[tile(d), whole(grads), whole(grads)],
            scratch_shapes=[
                pltpu.VMEM((count, latw), BF16),
                pltpu.VMEM((8, d), F32),
                pltpu.VMEM(ku.shape, F32),
                pltpu.VMEM(vu.shape, F32),
            ],
        ),
        out_shape=[shape_of((count, d), BF16), shape_of(grads, BF16), shape_of(grads, BF16)],
        cost_estimate=cost(17),
        compiler_params=params(),
        name="project_back",
    )(core, *gq, *gk, *gv, latt, nt_, tokens, ghid, first, first, ku, vu, gains, gn_mid)


def swap(values, axis_name, bit):
    size = lax.axis_size(axis_name)
    return lax.ppermute(values, axis_name, [(i, i ^ bit) for i in range(size)])


def bits_of(axis_name):
    size = lax.axis_size(axis_name)
    return [1 << i for i in range(size.bit_length() - 1)]


def owner_bits():
    names = [("dp", bit) for bit in reversed(bits_of("dp")) if bit > 1]
    return names + [("fsdp", bit) for bit in reversed(bits_of("fsdp"))]


def add(a, b, dtype=BF16):
    return (a.astype(F32) + b.astype(F32)).astype(dtype)


def part_of(values, names, which, mine, trail=2):
    axis_name, bit = which
    own = (lax.axis_index(axis_name) // bit) % 2
    at = values.ndim - trail - len(names) + names.index(which)
    return lax.dynamic_index_in_dim(values, own if mine else 1 - own, at, keepdims=False)


def scatter_rounds(keep, send):
    (came,) = yield [(send, "dp", 1)]
    names = owner_bits()
    rows = keep.size // (2 * keep.shape[-1]) >> len(names)
    shape = (2,) * len(names) + (rows, keep.shape[-1])
    keep, came = keep.reshape((2,) + shape), came.reshape((2,) + shape)
    firsts = [("fsdp", 1), ("dp", 2)]
    parts = [(keep[0], came[0]), (keep[1], came[1])]
    left = [names, names]
    for orders in (firsts, firsts[::-1]):
        split = [
            [add(*(part_of(x, kept, which, mine) for x in part)) for mine in (False, True)]
            for part, kept, which in zip(parts, left, orders)
        ]
        come = yield [(send, *which) for (send, _), which in zip(split, orders)]
        parts = [(keep, here) for (_, keep), here in zip(split, come)]
        left = [
            [name for name in kept if name != which] for kept, which in zip(left, orders)
        ]
    both, names = jnp.stack([add(*part) for part in parts]), left[0]
    rest = sorted(names, key=lambda name: (name[0] != "fsdp", name[1]))
    for which in rest:
        (came,) = yield [(part_of(both, names, which, False), *which)]
        both = add(
            part_of(both, names, which, True), came, F32 if which == rest[-1] else BF16
        )
        names = [name for name in names if name != which]
    return both


def gather_rounds(values):
    names = owner_bits()
    firsts = [("fsdp", 1), ("dp", 2)]
    rest = [name for name in names if name not in firsts]
    rest = sorted(rest, key=lambda name: (name[0] != "fsdp", name[1]), reverse=True)
    every = [("dp", 1 << i) for i in reversed(range(len(bits_of("dp"))))]
    every += [("fsdp", 1 << i) for i in reversed(range(len(bits_of("fsdp"))))]

    def join(part, came, have, which):
        have = sorted(have + [which], key=every.index)
        axis_name, bit = which
        low = (lax.axis_index(axis_name) // bit) % 2 == 0
        pair = (jnp.where(low, part, came), jnp.where(low, came, part))
        return jnp.stack(pair, axis=have.index(which)), have

    have = []
    for which in rest:
        (came,) = yield [(values, *which)]
        values, have = join(values, came, have, which)
    cut = values.shape[-1] // 256 * 128
    parts = [values[..., :cut], values[..., cut:]]
    haves = [have, have]
    for orders in (firsts, firsts[::-1], [("dp", 1)] * 2):
        come = yield [(part, *which) for part, which in zip(parts, orders)]
        both = [join(*item) for item in zip(parts, come, haves, orders)]
        parts, haves = [x[0] for x in both], [x[1] for x in both]
    whole_ = jnp.concatenate(parts, axis=-1)
    return whole_.reshape(-1, whole_.shape[-1])


class Rounds:
    def __init__(self, steps):
        self.steps = steps
        self.wants = next(self.steps)
        self.done = None

    def after(self, other):
        values = [want[0] for want in self.wants]
        values, _ = lax.optimization_barrier((values, [want[0] for want in other.wants]))
        self.wants = [(value, *want[1:]) for value, want in zip(values, self.wants)]

    def take(self, come):
        try:
            self.wants = self.steps.send(come)
        except StopIteration as end:
            self.wants, self.done = [], end.value


def beside(held, runs, work):
    sends = [[want[0] for want in run.wants] for run in runs]
    held, sends = lax.optimization_barrier((held, sends))
    come = [
        [swap(values, *want[1:]) for values, want in zip(group, run.wants)]
        for group, run in zip(sends, runs)
    ]
    result = work(held)
    result, come = lax.optimization_barrier((result, come))
    for run, here in zip(runs, come):
        run.take(here)
    return result


def together(runs):
    beside((), runs, lambda held: held)


def finish(runs):
    while any(run.wants for run in runs):
        live = [run for run in runs if run.wants]
        come = [[swap(*want) for want in run.wants] for run in live]
        for run, here in zip(live, come):
            run.take(here)


def shards(
    tokens,
    doc_ids,
    norm_in,
    query_weight,
    latent_weight,
    key_up_weight,
    value_up_weight,
    output_weight,
    norm_mid,
    gate_weight,
    up_weight,
    down_weight,
    cotangent,
):
    both = ("dp", "fsdp")
    n_dp = lax.axis_size("dp")
    devices = n_dp * lax.axis_size("fsdp")
    own_rows, d = query_weight.shape
    d_all = own_rows * devices
    latw = latent_weight.shape[1]
    up_rows, up_width = key_up_weight.shape
    ff = gate_weight.shape[1]

    gains = jnp.stack([norm_in, norm_mid], axis=1)
    gains = jnp.pad(gains, ((0, 0), (0, PAIR - 2)))
    packed = jnp.concatenate(
        [
            query_weight,
            output_weight,
            latent_weight,
            jnp.concatenate([key_up_weight, value_up_weight], axis=0),
            gains,
        ],
        axis=1,
    )
    steps = ff // TILE
    cut = (steps + 1) // 2
    down_rows = down_weight.shape[0]
    folds = -(-down_rows // own_rows)
    down_own = jnp.pad(down_weight, ((0, folds * own_rows - down_rows), (0, 0)))
    wide = jnp.concatenate(
        [down_own[i * own_rows : (i + 1) * own_rows] for i in range(folds)]
        + [gate_weight, up_weight],
        axis=1,
    )
    gate_at = folds * d // TILE
    get_first = Rounds(gather_rounds(packed))
    for _ in range(0):
        together([get_first])
    wide = beside(wide, [get_first], lambda held: held)
    wide = lax.all_gather(wide, both, axis=0, tiled=True)
    while get_first.wants:
        together([get_first])
    first = get_first.done

    at = 2 * d + latw
    ups = first[:, at : at + up_width].reshape(devices, 2, up_rows, up_width)
    ku = ups[:, 0].reshape(devices * up_rows, up_width)
    vu = ups[:, 1].reshape(devices * up_rows, up_width)
    mask = visible(doc_ids)
    core = (lax.axis_index("dp") % 2).astype(jnp.int32).reshape(1)

    q, lat, latt, k, v, normed_t, gain_rows = project(tokens, first, ku, vu)
    pairs = q.shape[1] // PAIR
    halves = [attend(mask, q, k, v, 0, pairs)]
    wo = (first, pl.BlockSpec((d_all, d), lambda i, *_: (0, 1)))
    hid, mid, midt = middle([half[0] for half in halves], wo, tokens, gain_rows)
    down = unfold(wide, own_rows, down_rows, d)
    out, gmid, keep_a, send_a, gdown = feed(
        core, mid, midt, cotangent, hid, None, (wide, gate_at), (wide, gate_at + steps), down, (0, cut), 0, n_dp, ff
    )
    lead = d // 2
    run_a = Rounds(scatter_rounds(keep_a, send_a))
    layer_out, gmid, keep_b, send_b, gdown = beside(
        out,
        [run_a],
        lambda out: feed(
            core,
            mid,
            midt,
            cotangent,
            out,
            (gmid, gdown),
            (wide, gate_at),
            (wide, gate_at + steps),
            down,
            (cut, steps),
            lead,
            n_dp,
            ff,
        ),
    )
    split = gdown.reshape(2, n_dp // 2, 2, ff // n_dp, d // 2)
    run_d = Rounds(
        scatter_rounds(
            lax.dynamic_index_in_dim(split, core[0], 2, keepdims=False),
            lax.dynamic_index_in_dim(split, 1 - core[0], 2, keepdims=False),
        )
    )
    ghid, gatt, keep_b, send_b, gnorm_mid = beside(
        gmid,
        [run_a, run_d],
        lambda gmid: middle_back(
            core,
            gmid,
            hid,
            cotangent,
            [half[1] for half in halves],
            wo,
            gain_rows,
            keep_b,
            send_b,
        ),
    )
    run_b = Rounds(scatter_rounds(keep_b, send_b))
    gq, gk, gv = [], [], []
    plan = ([run_a, run_b], [run_d, run_a], [run_b, run_a], [run_b, run_d])
    each = pairs // len(plan)
    for part, runs in enumerate(plan):
        half = halves[part * len(halves) // len(plan)]
        at = part * each % (pairs // len(halves))
        pieces = beside(
            gatt,
            runs,
            lambda gatt: attend_back(
                mask, q, k, v, half[0], gatt, half[2], part * each, at, each
            ),
        )
        for kept, piece in zip((gq, gk, gv), pieces):
            kept.append(piece)
    gtok, keep_c, send_c = beside(
        ghid,
        [run_b, run_d],
        lambda ghid: project_back(
            core,
            gq,
            gk,
            gv,
            latt,
            normed_t,
            tokens,
            ghid,
            first,
            ku,
            vu,
            gain_rows,
            gnorm_mid,
            n_dp,
            up_rows,
        ),
    )
    run_c = Rounds(scatter_rounds(keep_c, send_c))
    last = [run_b, run_d]
    come = [[swap(*want) for want in run.wants] for run in last]
    for _ in range(3):
        together([run_c])
    kept, come = lax.optimization_barrier(([want[0] for want in run_c.wants], come))
    run_c.wants = [(value, *want[1:]) for value, want in zip(kept, run_c.wants)]
    finish([run_c])
    for run, here in zip(last, come):
        run.take(here)
    finish([run_a, run_b, run_d])
    s_a, s_b, s_c, s_down = (run.done for run in (run_a, run_b, run_c, run_d))
    merge = lambda a, b: jnp.concatenate([a, b], axis=1)
    return (
        layer_out,
        gtok,
        s_c[0, :, d],
        s_c[0, :, :d],
        s_c[1, :, :latw],
        s_c[1, :up_rows, latw : latw + up_width],
        s_c[1, up_rows:, latw : latw + up_width],
        merge(s_b[0, :, :lead], s_b[1, :, :lead]),
        s_c[1, :, d],
        merge(s_a[0], s_b[0, :, lead:]),
        merge(s_a[1], s_b[1, :, lead:]),
        merge(s_down[0], s_down[1]),
    )


def solution(mesh):
    split = ("dp", "fsdp")
    flat, matrix = P(split), P(split, None)
    return jax.shard_map(
        shards,
        mesh=mesh,
        in_specs=(
            matrix,
            matrix,
            flat,
            matrix,
            matrix,
            matrix,
            matrix,
            matrix,
            flat,
            matrix,
            matrix,
            matrix,
            matrix,
        ),
        out_specs=(
            matrix,
            matrix,
            flat,
            matrix,
            matrix,
            matrix,
            matrix,
            matrix,
            flat,
            matrix,
            matrix,
            matrix,
        ),
        check_vma=False,
    )
```

```python
import functools

import jax
import jax.numpy as jnp
from jax import lax
from jax.experimental import pallas as pl
from jax.experimental.pallas import tpu as pltpu
from jax.sharding import PartitionSpec as P

HD = 64
G = 2
HG = 8
PAIR = 128
EPSILON = 1e-05
SCORE_SCALE = 0.125
NEGATIVE = -1e30
LOG2E = 1.4426950408889634
F32 = jnp.float32
BF16 = jnp.bfloat16
TILE = 256
QT = 128
SPAN = 4
PP = 2
PPB = 2
VMEM_LIMIT = 60 * 1024 * 1024


def nn(a, b):
    return lax.dot_general(a, b, (((1,), (0,)), ((), ())), preferred_element_type=F32)


def nt(a, b):
    return lax.dot_general(a, b, (((1,), (1,)), ((), ())), preferred_element_type=F32)


def tn(a, b):
    return lax.dot_general(a, b, (((0,), (0,)), ((), ())), preferred_element_type=F32)


def params(**extra):
    return pltpu.CompilerParams(vmem_limit_bytes=VMEM_LIMIT, **extra)


def whole(shape):
    return pl.BlockSpec(shape, lambda *_: (0,) * len(shape))


def rows_of(tile, width):
    return pl.BlockSpec((tile, width), lambda i: (i, 0))


def cost(micros):
    return pl.CostEstimate(flops=int(micros * 1.1e9), bytes_accessed=0, transcendentals=0)


def shape_of(shape, dtype):
    return jax.ShapeDtypeStruct(shape, dtype)


def project_kernel(
    tok_ref,
    wq_ref,
    wl_ref,
    wg_ref,
    ku_ref,
    vu_ref,
    q_ref,
    lat_ref,
    latt_ref,
    k_ref,
    v_ref,
    nt_ref,
    gain_ref,
):
    @pl.when(pl.program_id(0) == 0)
    def _():
        gain_ref[...] = wg_ref[...].astype(F32).T[0:8, :]

    x = tok_ref[...].astype(F32)
    root = lax.rsqrt(jnp.mean(x * x, axis=-1, keepdims=True) + EPSILON)
    normed = (x * root * gain_ref[0:1, :]).astype(BF16)
    nt_ref[...] = normed.T
    lat = nn(normed, wl_ref[...]).astype(BF16)
    lat_ref[...] = lat
    latt_ref[...] = lat.T
    q_ref[...] = (nn(normed, wq_ref[...]).astype(BF16).astype(F32) * SCORE_SCALE).astype(BF16)
    wide = lat.shape[1] // G
    out = k_ref.shape[1] // G
    for g in range(G):
        piece = lat[:, g * wide : (g + 1) * wide]
        k_ref[:, g * out : (g + 1) * out] = nn(
            piece, ku_ref[g * wide : (g + 1) * wide, :]
        ).astype(BF16)
        v_ref[:, g * out : (g + 1) * out] = nn(
            piece, vu_ref[g * wide : (g + 1) * wide, :]
        ).astype(BF16)


def columns_of(height, tile):
    return pl.BlockSpec((height, tile), lambda i: (0, i))


def project(tokens, first, ku, vu):
    count, d = tokens.shape
    latw = ku.shape[0]
    width = G * ku.shape[1]
    return pl.pallas_call(
        project_kernel,
        grid=(count // TILE,),
        in_specs=[
            rows_of(TILE, d),
            pl.BlockSpec((d, width), lambda i: (0, 0)),
            pl.BlockSpec((d, latw), lambda i: (0, (width + d) // latw)),
            pl.BlockSpec((d, PAIR), lambda i: (0, (width + d + 2 * latw) // PAIR)),
            whole(ku.shape),
            whole(vu.shape),
        ],
        out_specs=[
            rows_of(TILE, width),
            rows_of(TILE, latw),
            columns_of(latw, TILE),
            rows_of(TILE, width),
            rows_of(TILE, width),
            columns_of(d, TILE),
            whole((8, d)),
        ],
        out_shape=[
            shape_of((count, width), BF16),
            shape_of((count, latw), BF16),
            shape_of((latw, count), BF16),
            shape_of((count, width), BF16),
            shape_of((count, width), BF16),
            shape_of((d, count), BF16),
            shape_of((8, d), F32),
        ],
        cost_estimate=cost(10),
        compiler_params=params(),
        name="project",
    )(tokens, first, first, first, ku, vu)


def visible(doc):
    length = doc.shape[1]
    ids = doc.reshape(length)
    blocks = []
    padded = jnp.concatenate([jnp.full((SPAN * QT,), -1, ids.dtype), ids])
    for b in range(length // QT):
        keys = jnp.arange((b - SPAN) * QT, (b + 1) * QT)
        own = ids[b * QT : (b + 1) * QT]
        theirs = padded[b * QT : (b + SPAN + 1) * QT]
        queries = jnp.arange(b * QT, (b + 1) * QT)
        seen = (theirs[:, None] == own[None, :]) & (keys[:, None] <= queries[None, :])
        blocks.append(jnp.where(seen, 0.0, NEGATIVE))
    return jnp.stack(blocks).astype(BF16)


def split_heads(values):
    low = lax.broadcasted_iota(jnp.int32, values.shape, 1) < HD
    zero = jnp.zeros_like(values)
    return jnp.concatenate([jnp.where(low, values, zero), jnp.where(low, zero, values)], axis=0)


def attend_kernel(q_ref, k_ref, v_ref, mask_ref, o_ref, ot_ref, lse_ref):
    length = q_ref.shape[0]
    low = lax.broadcasted_iota(jnp.int32, (QT, PAIR), 1) < HD
    for b in range(length // QT):
        rows = slice(b * QT, (b + 1) * QT)
        extra = min(b, SPAN)
        keys = slice((b - extra) * QT, (b + 1) * QT)
        bias = mask_ref[b, (SPAN - extra) * QT :, :].astype(F32)
        bias = jnp.concatenate([bias, bias], axis=1)
        for pair in range(PP):
            cols = slice(pair * PAIR, (pair + 1) * PAIR)
            s = nt(k_ref[keys, cols], split_heads(q_ref[rows, cols])) * LOG2E + bias
            top = jnp.max(s, axis=0, keepdims=True)
            p = jnp.exp2(s - top).astype(BF16)
            v = v_ref[keys, cols]
            r = tn(p, jnp.concatenate([v, jnp.ones_like(v)], axis=1))
            r = jnp.where(
                jnp.concatenate([low, low], axis=1), r[:QT], r[QT:]
            )
            o = r[:, :PAIR] / r[:, PAIR:]
            o_ref[rows, cols] = o.astype(BF16)
            ot_ref[cols, rows] = o.T.astype(BF16)
            total = jnp.log2(r[:, PAIR:].T)
            lse_ref[pair, 0:1, rows] = top[:, :QT] + total[0:1]
            lse_ref[pair, 1:2, rows] = top[:, QT:] + total[HD : HD + 1]


def attend(mask, q, k, v, start, pairs):
    length = q.shape[0]
    width = pairs * PAIR
    wide = PP * PAIR
    strip = pl.BlockSpec((length, wide), lambda i: (0, start // PP + i))
    return pl.pallas_call(
        attend_kernel,
        grid_spec=pltpu.PrefetchScalarGridSpec(
            num_scalar_prefetch=0,
            grid=(pairs // PP,),
            in_specs=[strip, strip, strip, whole(mask.shape)],
            out_specs=[
                pl.BlockSpec((length, wide), lambda i: (0, i)),
                pl.BlockSpec((wide, length), lambda i: (i, 0)),
                pl.BlockSpec((PP, 8, length), lambda i: (i, 0, 0)),
            ],
        ),
        out_shape=[
            shape_of((length, width), BF16),
            shape_of((width, length), BF16),
            shape_of((pairs, 8, length), F32),
        ],
        cost_estimate=cost(2.5 * pairs),
        compiler_params=params(),
        name="attend",
    )(q, k, v, mask)


def attend_back_kernel(
    q_ref,
    k_ref,
    v_ref,
    o_ref,
    do_ref,
    lse_ref,
    mask_ref,
    dq_ref,
    dk_ref,
    dv_ref,
    dk_acc,
    dv_acc,
):
    length = q_ref.shape[0]
    low = lax.broadcasted_iota(jnp.int32, (QT, PAIR), 1) < HD
    dk_acc[...] = jnp.zeros_like(dk_acc)
    dv_acc[...] = jnp.zeros_like(dv_acc)
    kts = [k_ref[:, pair * PAIR : (pair + 1) * PAIR].T for pair in range(PPB)]
    for b in range(length // QT):
        rows = slice(b * QT, (b + 1) * QT)
        extra = min(b, SPAN)
        keys = slice((b - extra) * QT, (b + 1) * QT)
        bias = mask_ref[b, (SPAN - extra) * QT :, :].astype(F32)
        bias = jnp.concatenate([bias, bias], axis=1)
        for pair in range(PPB):
            cols = slice(pair * PAIR, (pair + 1) * PAIR)
            do = do_ref[rows, cols]
            prod = (do.astype(F32) * o_ref[rows, cols].astype(F32)).T
            inner = jnp.concatenate(
                [
                    jnp.sum(prod[:HD], axis=0, keepdims=True),
                    jnp.sum(prod[HD:], axis=0, keepdims=True),
                ],
                axis=1,
            )
            lse = jnp.concatenate(
                [lse_ref[pair, 0:1, rows], lse_ref[pair, 1:2, rows]], axis=1
            )
            qs = split_heads(q_ref[rows, cols])
            dos = split_heads(do)
            k = k_ref[keys, cols]
            p = jnp.exp2(nt(k, qs) * LOG2E + bias - lse)
            ds = (p * (nt(v_ref[keys, cols], dos) - inner)).astype(BF16)
            dv_acc[keys, cols] += nn(p.astype(BF16), dos)
            dk_acc[keys, cols] += nn(ds, qs)
            dq = nn(kts[pair][:, keys], ds) * SCORE_SCALE
            dq = jnp.concatenate([dq[:HD, :QT], dq[HD:, QT:]], axis=0)
            dq_ref[rows, cols] = dq.T.astype(BF16)
    dk_ref[...] = dk_acc[...].astype(BF16)
    dv_ref[...] = dv_acc[...].astype(BF16)


def attend_back(mask, q, k, v, o, do, lse, start, at, pairs):
    length = q.shape[0]
    width = pairs * PAIR
    wide = PPB * PAIR
    strip = pl.BlockSpec((length, wide), lambda i: (0, start // PPB + i))
    own = pl.BlockSpec((length, wide), lambda i: (0, i))
    return pl.pallas_call(
        attend_back_kernel,
        grid_spec=pltpu.PrefetchScalarGridSpec(
            num_scalar_prefetch=0,
            grid=(pairs // PPB,),
            in_specs=[
                strip,
                strip,
                strip,
                pl.BlockSpec((length, wide), lambda i: (0, at // PPB + i)),
                strip,
                pl.BlockSpec((PPB, 8, length), lambda i: (at // PPB + i, 0, 0)),
                whole(mask.shape),
            ],
            out_specs=[own] * 3,
            scratch_shapes=[
                pltpu.VMEM((length, wide), F32),
                pltpu.VMEM((length, wide), F32),
            ],
        ),
        out_shape=[shape_of((length, width), BF16)] * 3,
        cost_estimate=cost(3.5 * pairs),
        compiler_params=params(),
        name="attend_back",
    )(q, k, v, o, do, lse, mask)


def middle_kernel(*refs):
    att_refs = refs[:-6]
    wo_ref, tok_ref, gain_ref, hid_ref, mid_ref, midt_ref = refs[-6:]
    att = jnp.concatenate([ref[...] for ref in att_refs], axis=1)
    hid = tok_ref[...].astype(F32) + nn(att, wo_ref[...])
    hid_ref[...] = hid
    root = lax.rsqrt(jnp.mean(hid * hid, axis=-1, keepdims=True) + EPSILON)
    mid = (hid * root * gain_ref[1:2, :]).astype(BF16)
    mid_ref[...] = mid
    midt_ref[...] = mid.T


def middle(att, wo, tokens, gains):
    count, d = tokens.shape
    return pl.pallas_call(
        middle_kernel,
        grid=(count // TILE,),
        in_specs=[rows_of(TILE, x.shape[1]) for x in att]
        + [wo[1], rows_of(TILE, d), whole((8, d))],
        out_specs=[rows_of(TILE, d), rows_of(TILE, d), columns_of(d, TILE)],
        out_shape=[
            shape_of((count, d), F32),
            shape_of((count, d), BF16),
            shape_of((d, count), BF16),
        ],
        cost_estimate=cost(8),
        compiler_params=params(),
        name="middle",
    )(*att, wo[0], tokens, gains)


def unfold_kernel(own_rows, down_rows, in_ref, out_ref):
    d = out_ref.shape[1]
    for device in range(in_ref.shape[0] // own_rows):
        for fold in range(in_ref.shape[1] // d):
            count = min(own_rows, down_rows - fold * own_rows)
            at = device * down_rows + fold * own_rows
            out_ref[at : at + count, :] = in_ref[
                device * own_rows : device * own_rows + count, fold * d : (fold + 1) * d
            ]


def unfold(wide, own_rows, down_rows, d):
    folds = -(-down_rows // own_rows)
    devices = wide.shape[0] // own_rows
    if own_rows % 16 or devices % 8:
        down = wide[:, : folds * d].reshape(devices, own_rows, folds, d).transpose(0, 2, 1, 3)
        down = down.reshape(devices, folds * own_rows, d)[:, :down_rows]
        return down.reshape(devices * down_rows, d)
    return pl.pallas_call(
        functools.partial(unfold_kernel, own_rows, down_rows),
        grid=(devices // 8,),
        in_specs=[pl.BlockSpec((8 * own_rows, folds * d), lambda i: (i, 0))],
        out_specs=pl.BlockSpec((8 * down_rows, d), lambda i: (i, 0)),
        out_shape=shape_of((devices * down_rows, d), BF16),
        cost_estimate=cost(5),
        compiler_params=params(),
        name="unfold",
    )(wide)


def owner_rows(core_ref, pair, height, mine, span=None):
    core = core_ref[0]
    first = 2 * pair if span is None else 2 * pair % span
    which = first + (core if mine else 1 - core)
    return pl.ds(pl.multiple_of(which * height, height), height)


def feed_kernel(first, core_ref, *refs):
    refs = list(refs)
    mid_ref, midt_ref, cot_ref = refs[:3]
    del refs[:3]
    gfrom_ref = None
    if not first:
        gfrom_ref = refs[0]
        del refs[:2]
    gate_ref, up_ref, down_ref, gmid_ref, act_ref, keep_ref, send_ref, gdown_ref = refs[:8]
    gmid_acc, act_s, ggp_s, gup_s, gp_s, up_s, ga_s = refs[8:]

    @pl.when(pl.program_id(0) == 0)
    def _():
        if first:
            gmid_acc[...] = jnp.zeros_like(gmid_acc)
        else:
            gmid_acc[...] = gfrom_ref[...]

    gate = gate_ref[...]
    up = up_ref[...]

    slot = pl.program_id(0) % 2
    steps = pl.num_programs(0) - 1
    _, pairs, height, _ = keep_ref.shape
    half = cot_ref.shape[1] // 2

    count = mid_ref.shape[0]
    tile = count // 4

    def products():
        m = mid_ref[...]
        gp_s[...] = nn(m, gate)
        up_s[...] = nn(m, up)
        ga_s[...] = nt(cot_ref[...], down_ref[...])

    def pointwise(r):
        rows = slice(r * tile, (r + 1) * tile)
        gate_pre, up_pre, grad_act = gp_s[rows, :], up_s[rows, :], ga_s[rows, :]
        sig = 0.5 * jnp.tanh(0.5 * gate_pre) + 0.5
        silu = gate_pre * sig
        act = (silu * up_pre).astype(BF16)
        act_ref[rows, :] = act
        act_s[slot, rows, :] = act
        ggp_s[slot, rows, :] = (grad_act * up_pre * (sig + silu * (1.0 - sig))).astype(BF16)
        gup_s[slot, rows, :] = (grad_act * silu).astype(BF16)

    def sums():
        gmid_acc[...] += nt(ggp_s[slot], gate) + nt(gup_s[slot], up)

    def grads(r):
        ggp, gup, act = ggp_s[1 - slot], gup_s[1 - slot], act_s[1 - slot]
        mine, ref = ((False, send_ref), (True, keep_ref))[r % 2]
        if r < 2:
            rows = [midt_ref[owner_rows(core_ref, p, height, mine), :] for p in range(pairs)]
            m = jnp.concatenate(rows, axis=0)
            ref[0] = nn(m, ggp).astype(BF16).reshape(ref.shape[1:])
            ref[1] = nn(m, gup).astype(BF16).reshape(ref.shape[1:])
        else:
            cols = slice((r - 2) * half, (r - 1) * half)
            gdown_ref[r - 2] = tn(act, cot_ref[:, cols]).astype(BF16)

    def first_half():
        products()
        for r in range(4):
            pointwise(r)
        sums()

    def second_half():
        for r in range(4):
            grads(r)

    def both_halves():
        products()
        for r in range(4):
            grads(r)
            pointwise(r)
        sums()

    @pl.when(pl.program_id(0) == 0)
    def _():
        first_half()

    @pl.when((pl.program_id(0) > 0) & (pl.program_id(0) < steps))
    def _():
        both_halves()

    @pl.when(pl.program_id(0) == steps)
    def _():
        second_half()

    @pl.when(pl.program_id(0) == pl.num_programs(0) - 1)
    def _():
        gmid_ref[...] = gmid_acc[...]


def feed(core, mid, midt, cot, before, gate, up, down, span, lead, n_dp, ff):
    count, d = mid.shape
    first = before is None
    at, steps = span[0], span[1] - span[0]
    args = [mid, midt, cot]
    specs = [whole((count, d)), whole((d, count)), whole((count, d))]
    alias = {}
    if not first:
        args += list(before)
        specs += [whole((count, d)), pl.BlockSpec(memory_space=pl.ANY)]
        alias = {5: 4}
    height = d // n_dp
    now = lambda i: jnp.minimum(i, steps - 1)
    past = lambda i: jnp.maximum(i - 1, 0)
    strip = pl.BlockSpec((2, n_dp // 2, height, TILE), lambda i, *_: (0, 0, 0, past(i) + lead // TILE))
    grads = shape_of((2, n_dp // 2, height, lead + steps * TILE), BF16)
    return pl.pallas_call(
        functools.partial(feed_kernel, first),
        grid_spec=pltpu.PrefetchScalarGridSpec(
            num_scalar_prefetch=1,
            grid=(steps + 1,),
            in_specs=specs
            + [
                pl.BlockSpec((d, TILE), lambda i, *_: (0, gate[1] + at + now(i))),
                pl.BlockSpec((d, TILE), lambda i, *_: (0, up[1] + at + now(i))),
                pl.BlockSpec((TILE, d), lambda i, *_: (at + now(i), 0)),
            ],
            out_specs=[
                whole((count, d)),
                pl.BlockSpec((count, TILE), lambda i, *_: (0, now(i))),
                strip,
                strip,
                pl.BlockSpec((2, TILE, d // 2), lambda i, *_: (0, at + past(i), 0)),
            ],
            scratch_shapes=[pltpu.VMEM((count, d), F32)]
            + [pltpu.VMEM((2, count, TILE), BF16)] * 3
            + [pltpu.VMEM((count, TILE), F32)] * 3,
        ),
        out_shape=[
            shape_of((count, d), F32),
            shape_of((count, steps * TILE), BF16),
            grads,
            grads,
            shape_of((2, ff, d // 2), BF16),
        ],
        input_output_aliases=alias,
        cost_estimate=cost(5.5 * steps),
        compiler_params=params(),
        name="feed",
    )(core, *args, gate[0], up[0], down)


def leave_kernel(hid_ref, *refs):
    act_refs, down_ref, out_ref = refs[:-2], refs[-2], refs[-1]
    total = hid_ref[...]
    at = 0
    for ref in act_refs:
        wide = ref.shape[1]
        total += nn(ref[...], down_ref[at : at + wide, :])
        at += wide
    out_ref[...] = total.astype(BF16)


def leave(hid, acts, down):
    count, d = hid.shape
    tile = 2 * TILE
    return pl.pallas_call(
        leave_kernel,
        grid=(count // tile,),
        in_specs=[rows_of(tile, d)] + [rows_of(tile, x.shape[1]) for x in acts] + [whole(down.shape)],
        out_specs=rows_of(tile, d),
        out_shape=shape_of((count, d), BF16),
        cost_estimate=cost(9),
        compiler_params=params(),
        name="leave",
    )(hid, *acts, down)


def middle_back_kernel(
    core_ref,
    gmid_ref,
    hid_ref,
    cot_ref,
    *refs,
):
    attt_refs = refs[:-10]
    (
        wo_ref,
        gain_ref,
        keep_in,
        send_in,
        ghid_ref,
        gatt_ref,
        keep_ref,
        send_ref,
        gn_ref,
        branch_s,
    ) = refs[-10:]
    step = pl.program_id(0)
    tile = hid_ref.shape[0]

    @pl.when(step == 0)
    def _():
        gn_ref[...] = jnp.zeros_like(gn_ref)

    hid = hid_ref[...]
    root = lax.rsqrt(jnp.mean(hid * hid, axis=-1, keepdims=True) + EPSILON)
    unit = hid * root
    gmid = gmid_ref[...]
    gn_ref[0:1, :] += jnp.sum(gmid * unit, axis=0, keepdims=True)
    t = gmid * gain_ref[1:2, :]
    inner = jnp.mean(t * unit, axis=-1, keepdims=True)
    ghid = cot_ref[...].astype(F32) + root * (t - unit * inner)
    ghid_ref[...] = ghid
    branch = ghid.astype(BF16)
    gatt_ref[...] = nt(branch, wo_ref[...]).astype(BF16)
    branch_s[pl.ds(pl.multiple_of(step * tile, tile), tile), :] = branch

    @pl.when(step == pl.num_programs(0) - 1)
    def _():
        half = branch_s.shape[1] // 2
        _, pairs, height, _ = keep_ref.shape
        tall = attt_refs[0].shape[0]
        for p in range(pairs):
            for mine, ref in ((False, send_ref), (True, keep_ref)):
                attt_ref = attt_refs[2 * p * height // tall]
                rows = attt_ref[owner_rows(core_ref, p, height, mine, tall // height), :]
                grad = nn(rows, branch_s[...]).astype(BF16)
                ref[0, p] = grad[:, :half]
                ref[1, p] = grad[:, half:]


def middle_back(core, gmid, hid, cot, attt, wo, gains, keep, send):
    count, d = hid.shape
    width = sum(x.shape[0] for x in attt)
    pairs, height = keep.shape[1:3]
    anywhere = pl.BlockSpec(memory_space=pl.ANY)
    strip = pl.BlockSpec((2, pairs, height, d // 2), lambda i, *_: (0, 0, 0, 0))
    tile = lambda wide: pl.BlockSpec((TILE, wide), lambda i, *_: (i, 0))
    return pl.pallas_call(
        middle_back_kernel,
        grid_spec=pltpu.PrefetchScalarGridSpec(
            num_scalar_prefetch=1,
            grid=(count // TILE,),
            in_specs=[
                tile(d),
                tile(d),
                tile(d),
            ]
            + [whole(x.shape) for x in attt]
            + [
                wo[1],
                whole((8, d)),
                anywhere,
                anywhere,
            ],
            out_specs=[tile(d), tile(width), strip, strip, whole((8, d))],
            scratch_shapes=[pltpu.VMEM((count, d), BF16)],
        ),
        out_shape=[
            shape_of((count, d), F32),
            shape_of((count, width), BF16),
            shape_of(keep.shape, BF16),
            shape_of(send.shape, BF16),
            shape_of((8, d), F32),
        ],
        input_output_aliases={6 + len(attt): 2, 7 + len(attt): 3},
        cost_estimate=cost(12),
        compiler_params=params(),
        name="middle_back",
    )(core, gmid, hid, cot, *attt, wo[0], gains, keep, send)


def interleave(up_rows, height):
    to = lax.broadcasted_iota(jnp.int32, (height, height), 0)
    start = lax.broadcasted_iota(jnp.int32, (height, height), 1)
    turn, row = to // (2 * up_rows), to % (2 * up_rows)
    late = (row >= up_rows).astype(jnp.int32)
    want = turn * up_rows + row - late * up_rows + late * (height // 2)
    return (start == want).astype(F32).astype(BF16)


def weights_back_kernel(up_rows, core_ref, *refs):
    parts = (len(refs) - 9) // 3
    gq_refs, gk_refs, gv_refs = refs[:parts], refs[parts : 2 * parts], refs[2 * parts : 3 * parts]
    latt_ref, nt_ref, ku_ref, vu_ref, glat_ref, keep_ref, send_ref, gku_s, gvu_s = refs[3 * parts :]
    wide = ku_ref.shape[0] // G
    out = ku_ref.shape[1]
    glats = [None] * G
    at = 0
    for part in range(parts):
        strip = gk_refs[part].shape[1]
        g, start = at // out, at % out
        own, cols = slice(g * wide, (g + 1) * wide), slice(start, start + strip)
        gk, gv = gk_refs[part][...], gv_refs[part][...]
        here = nt(gk, ku_ref[own, cols]) + nt(gv, vu_ref[own, cols])
        glats[g] = here if glats[g] is None else glats[g] + here
        gku_s[own, cols] = nn(latt_ref[own, :], gk)
        gvu_s[own, cols] = nn(latt_ref[own, :], gv)
        at += strip
    for g in range(G):
        glat_ref[:, g * wide : (g + 1) * wide] = glats[g].astype(BF16)
    _, pairs, height, _ = keep_ref.shape
    latw = glat_ref.shape[1]
    owners = height // (2 * up_rows)
    core = core_ref[0]
    for mine, ref in ((False, send_ref), (True, keep_ref)):
        rows = [nt_ref[owner_rows(core_ref, p, height, mine), :] for p in range(pairs)]
        m = jnp.concatenate(rows, axis=0)
        at = 0
        for gq_ref in gq_refs:
            strip = gq_ref.shape[1]
            grad = nn(m, gq_ref[...]).astype(BF16)
            ref[0, :, :, at : at + strip] = grad.reshape(pairs, height, strip)
            at += strip
        grad = nn(m, glat_ref[...]).astype(BF16)
        ref[1, :, :, 0:latw] = grad.reshape(pairs, height, latw)
        for p in range(pairs):
            which = 2 * p + (core if mine else 1 - core)
            near = pl.ds(pl.multiple_of(which * (height // 2), height // 2), height // 2)
            keys, values = gku_s[near, :], gvu_s[near, :]
            if up_rows % 8:
                both = jnp.concatenate([keys, values], axis=0).astype(BF16)
                ups = nn(interleave(up_rows, height), both)
            else:
                pieces = []
                for j in range(owners):
                    pieces.append(keys[j * up_rows : (j + 1) * up_rows])
                    pieces.append(values[j * up_rows : (j + 1) * up_rows])
                ups = jnp.concatenate(pieces, axis=0)
            ref[1, p, :, latw : latw + out] = ups.astype(BF16)


def weights_back(core, gq, gk, gv, latt, nt_, ku, vu, n_dp, up_rows):
    count = gq[0].shape[0]
    d = nt_.shape[0]
    width = sum(x.shape[1] for x in gq)
    latw = latt.shape[0]
    grads = (2, n_dp // 2, d // n_dp, width)
    args = [*gq, *gk, *gv, latt, nt_, ku, vu]
    return pl.pallas_call(
        functools.partial(weights_back_kernel, up_rows),
        grid_spec=pltpu.PrefetchScalarGridSpec(
            num_scalar_prefetch=1,
            grid=(1,),
            in_specs=[whole(x.shape) for x in args],
            out_specs=[whole((count, latw)), whole(grads), whole(grads)],
            scratch_shapes=[pltpu.VMEM(ku.shape, F32), pltpu.VMEM(vu.shape, F32)],
        ),
        out_shape=[shape_of((count, latw), BF16), shape_of(grads, BF16), shape_of(grads, BF16)],
        cost_estimate=cost(11),
        compiler_params=params(),
        name="weights_back",
    )(core, *args)


def tokens_back_kernel(*refs):
    glat_ref, tok_ref, ghid_ref, wq_ref, wl_ref, gain_ref, gtok_ref, gn_ref = refs[-8:]
    gq_refs = refs[:-8]

    @pl.when(pl.program_id(0) == 0)
    def _():
        gn_ref[...] = jnp.zeros_like(gn_ref)

    gq = jnp.concatenate([ref[...] for ref in gq_refs], axis=1)
    gin = nt(gq, wq_ref[...]) + nt(glat_ref[...], wl_ref[...])
    x = tok_ref[...].astype(F32)
    root = lax.rsqrt(jnp.mean(x * x, axis=-1, keepdims=True) + EPSILON)
    unit = x * root
    gn_ref[0:1, :] += jnp.sum(gin * unit, axis=0, keepdims=True)
    t = gin * gain_ref[0:1, :]
    inner = jnp.mean(t * unit, axis=-1, keepdims=True)
    gtok_ref[...] = (ghid_ref[...] + root * (t - unit * inner)).astype(BF16)


def tokens_back(gq, glat, tokens, ghid, first, gains):
    count, d = tokens.shape
    width = sum(x.shape[1] for x in gq)
    latw = glat.shape[1]
    return pl.pallas_call(
        tokens_back_kernel,
        grid=(count // TILE,),
        in_specs=[rows_of(TILE, x.shape[1]) for x in gq]
        + [
            rows_of(TILE, latw),
            rows_of(TILE, d),
            rows_of(TILE, d),
            pl.BlockSpec((d, width), lambda i: (0, 0)),
            pl.BlockSpec((d, latw), lambda i: (0, (width + d) // latw)),
            whole((8, d)),
        ],
        out_specs=[rows_of(TILE, d), whole((8, d))],
        out_shape=[shape_of((count, d), BF16), shape_of((8, d), F32)],
        cost_estimate=cost(8),
        compiler_params=params(),
        name="tokens_back",
    )(*gq, glat, tokens, ghid, first, first, gains)


def swap(values, axis_name, bit):
    size = lax.axis_size(axis_name)
    return lax.ppermute(values, axis_name, [(i, i ^ bit) for i in range(size)])


def bits_of(axis_name):
    size = lax.axis_size(axis_name)
    return [1 << i for i in range(size.bit_length() - 1)]


def owner_bits():
    names = [("dp", bit) for bit in reversed(bits_of("dp")) if bit > 1]
    return names + [("fsdp", bit) for bit in reversed(bits_of("fsdp"))]


def add(a, b, dtype=BF16):
    return (a.astype(F32) + b.astype(F32)).astype(dtype)


def part_of(values, names, which, mine, trail=2):
    axis_name, bit = which
    own = (lax.axis_index(axis_name) // bit) % 2
    at = values.ndim - trail - len(names) + names.index(which)
    return lax.dynamic_index_in_dim(values, own if mine else 1 - own, at, keepdims=False)


def scatter_rounds(keep, send):
    (came,) = yield [(send, "dp", 1)]
    names = owner_bits()
    rows = keep.size // (2 * keep.shape[-1]) >> len(names)
    shape = (2,) * len(names) + (rows, keep.shape[-1])
    keep, came = keep.reshape((2,) + shape), came.reshape((2,) + shape)
    firsts = [("fsdp", 1), ("dp", 2)]
    parts = [(keep[0], came[0]), (keep[1], came[1])]
    left = [names, names]
    for orders in (firsts, firsts[::-1]):
        split = [
            [add(*(part_of(x, kept, which, mine) for x in part)) for mine in (False, True)]
            for part, kept, which in zip(parts, left, orders)
        ]
        come = yield [(send, *which) for (send, _), which in zip(split, orders)]
        parts = [(keep, here) for (_, keep), here in zip(split, come)]
        left = [
            [name for name in kept if name != which] for kept, which in zip(left, orders)
        ]
    both, names = jnp.stack([add(*part) for part in parts]), left[0]
    rest = sorted(names, key=lambda name: (name[0] != "fsdp", name[1]))
    for which in rest:
        (came,) = yield [(part_of(both, names, which, False), *which)]
        both = add(
            part_of(both, names, which, True), came, F32 if which == rest[-1] else BF16
        )
        names = [name for name in names if name != which]
    return both


def gather_rounds(values):
    names = owner_bits()
    firsts = [("fsdp", 1), ("dp", 2)]
    rest = [name for name in names if name not in firsts]
    rest = sorted(rest, key=lambda name: (name[0] != "fsdp", name[1]), reverse=True)
    every = [("dp", 1 << i) for i in reversed(range(len(bits_of("dp"))))]
    every += [("fsdp", 1 << i) for i in reversed(range(len(bits_of("fsdp"))))]

    def join(part, came, have, which):
        have = sorted(have + [which], key=every.index)
        axis_name, bit = which
        low = (lax.axis_index(axis_name) // bit) % 2 == 0
        pair = (jnp.where(low, part, came), jnp.where(low, came, part))
        return jnp.stack(pair, axis=have.index(which)), have

    have = []
    for which in rest:
        (came,) = yield [(values, *which)]
        values, have = join(values, came, have, which)
    cut = values.shape[-1] // 256 * 128
    parts = [values[..., :cut], values[..., cut:]]
    haves = [have, have]
    for orders in (firsts, firsts[::-1], [("dp", 1)] * 2):
        come = yield [(part, *which) for part, which in zip(parts, orders)]
        both = [join(*item) for item in zip(parts, come, haves, orders)]
        parts, haves = [x[0] for x in both], [x[1] for x in both]
    whole_ = jnp.concatenate(parts, axis=-1)
    return whole_.reshape(-1, whole_.shape[-1])


class Rounds:
    def __init__(self, steps):
        self.steps = steps
        self.wants = next(self.steps)
        self.done = None

    def after(self, other):
        values = [want[0] for want in self.wants]
        values, _ = lax.optimization_barrier((values, [want[0] for want in other.wants]))
        self.wants = [(value, *want[1:]) for value, want in zip(values, self.wants)]

    def take(self, come):
        try:
            self.wants = self.steps.send(come)
        except StopIteration as end:
            self.wants, self.done = [], end.value


def beside(held, runs, work):
    sends = [[want[0] for want in run.wants] for run in runs]
    held, sends = lax.optimization_barrier((held, sends))
    come = [
        [swap(values, *want[1:]) for values, want in zip(group, run.wants)]
        for group, run in zip(sends, runs)
    ]
    result = work(held)
    result, come = lax.optimization_barrier((result, come))
    for run, here in zip(runs, come):
        run.take(here)
    return result


def together(runs):
    beside((), runs, lambda held: held)


def finish(runs):
    while any(run.wants for run in runs):
        live = [run for run in runs if run.wants]
        come = [[swap(*want) for want in run.wants] for run in live]
        for run, here in zip(live, come):
            run.take(here)


def shards(
    tokens,
    doc_ids,
    norm_in,
    query_weight,
    latent_weight,
    key_up_weight,
    value_up_weight,
    output_weight,
    norm_mid,
    gate_weight,
    up_weight,
    down_weight,
    cotangent,
):
    both = ("dp", "fsdp")
    n_dp = lax.axis_size("dp")
    devices = n_dp * lax.axis_size("fsdp")
    own_rows, d = query_weight.shape
    d_all = own_rows * devices
    latw = latent_weight.shape[1]
    up_rows, up_width = key_up_weight.shape
    ff = gate_weight.shape[1]

    gains = jnp.stack([norm_in, norm_mid], axis=1)
    gains = jnp.pad(gains, ((0, 0), (0, PAIR - 2)))
    packed = jnp.concatenate(
        [
            query_weight,
            output_weight,
            latent_weight,
            jnp.concatenate([key_up_weight, value_up_weight], axis=0),
            gains,
        ],
        axis=1,
    )
    steps = ff // TILE
    cut = (steps + 1) // 2
    down_rows = down_weight.shape[0]
    folds = -(-down_rows // own_rows)
    down_own = jnp.pad(down_weight, ((0, folds * own_rows - down_rows), (0, 0)))
    middle_at = cut * TILE
    wide = [
        jnp.concatenate(
            [down_own[i * own_rows : (i + 1) * own_rows] for i in range(folds)]
            + [gate_weight[:, :middle_at], up_weight[:, :middle_at]],
            axis=1,
        ),
        jnp.concatenate([gate_weight[:, middle_at:], up_weight[:, middle_at:]], axis=1),
    ]
    gate_at = folds * d // TILE
    get_first = Rounds(gather_rounds(packed))
    for _ in range(0):
        together([get_first])
    wide[0] = lax.all_gather(wide[0], both, axis=0, tiled=True)
    together([get_first])
    wide[1], _ = lax.optimization_barrier((wide[1], get_first.wants[0][0]))
    wide[1] = lax.all_gather(wide[1], both, axis=0, tiled=True)
    while get_first.wants:
        together([get_first])
    first = get_first.done

    at = 2 * d + latw
    ups = first[:, at : at + up_width].reshape(devices, 2, up_rows, up_width)
    ku = ups[:, 0].reshape(devices * up_rows, up_width)
    vu = ups[:, 1].reshape(devices * up_rows, up_width)
    mask = visible(doc_ids)
    core = (lax.axis_index("dp") % 2).astype(jnp.int32).reshape(1)

    q, lat, latt, k, v, normed_t, gain_rows = project(tokens, first, ku, vu)
    pairs = q.shape[1] // PAIR
    halves = [attend(mask, q, k, v, 0, pairs)]
    wo = (first, pl.BlockSpec((d_all, d), lambda i, *_: (0, 1)))
    hid, mid, midt = middle([half[0] for half in halves], wo, tokens, gain_rows)
    down = unfold(wide[0], own_rows, down_rows, d)
    gmid, act_a, keep_a, send_a, gdown = feed(
        core,
        mid,
        midt,
        cotangent,
        None,
        (wide[0], gate_at),
        (wide[0], gate_at + cut),
        down,
        (0, cut),
        0,
        n_dp,
        ff,
    )
    lead = d // 2
    run_a = Rounds(scatter_rounds(keep_a, send_a))
    gmid, act_b, keep_b, send_b, gdown = beside(
        gmid,
        [run_a],
        lambda gmid: feed(
            core,
            mid,
            midt,
            cotangent,
            (gmid, gdown),
            (wide[1], -cut),
            (wide[1], steps - 2 * cut),
            down,
            (cut, steps),
            lead,
            n_dp,
            ff,
        ),
    )
    split = gdown.reshape(2, n_dp // 2, 2, ff // n_dp, d // 2)
    run_d = Rounds(
        scatter_rounds(
            lax.dynamic_index_in_dim(split, core[0], 2, keepdims=False),
            lax.dynamic_index_in_dim(split, 1 - core[0], 2, keepdims=False),
        )
    )
    ghid, gatt, keep_b, send_b, gnorm_mid = beside(
        gmid,
        [run_a, run_d],
        lambda gmid: middle_back(
            core,
            gmid,
            hid,
            cotangent,
            [half[1] for half in halves],
            wo,
            gain_rows,
            keep_b,
            send_b,
        ),
    )
    run_b = Rounds(scatter_rounds(keep_b, send_b))
    gq, gk, gv = [], [], []
    half = halves[0]
    some = pairs // 4

    def attention_part(gatt, runs, start, count):
        pieces = beside(
            gatt,
            runs,
            lambda gatt: attend_back(
                mask, q, k, v, half[0], gatt, half[2], start, start, count
            ),
        )
        for kept, piece in zip((gq, gk, gv), pieces):
            kept.append(piece)

    attention_part(gatt, [run_a, run_b], 0, some)
    layer_out = beside(hid, [run_d, run_a], lambda hid: leave(hid, [act_a, act_b], down))
    attention_part(gatt, [run_d, run_a], some, some)
    attention_part(gatt, [run_b, run_d], 2 * some, pairs - 2 * some)
    glat, keep_c, send_c = beside(
        latt,
        [run_b, run_d],
        lambda latt: weights_back(
            core, gq, gk, gv, latt, normed_t, ku, vu, n_dp, up_rows
        ),
    )
    run_c = Rounds(scatter_rounds(keep_c, send_c))
    run_c.after(run_b)
    come = [swap(*want) for want in run_b.wants]
    together([run_c])
    come, _ = lax.optimization_barrier((come, [want[0] for want in run_c.wants]))
    run_b.take(come)
    come = [swap(*want) for want in run_b.wants]
    gtok, gnorm_in = beside(
        ghid, [run_c], lambda ghid: tokens_back(gq, glat, tokens, ghid, first, gain_rows)
    )
    kept, come = lax.optimization_barrier(([want[0] for want in run_c.wants], come))
    run_c.wants = [(value, *want[1:]) for value, want in zip(kept, run_c.wants)]
    gnorms = jnp.stack([gnorm_in[0], gnorm_mid[0]]).reshape(2, devices, own_rows)
    gnorms, _ = lax.optimization_barrier(
        (gnorms.transpose(1, 0, 2), [want[0] for want in run_c.wants])
    )
    gnorms = lax.all_to_all(gnorms, both, split_axis=0, concat_axis=0, tiled=True)
    together([run_c])
    while len(run_c.wants) > 0:
        gnorms = beside(gnorms, [run_c], lambda held: held)
    gnorms = jnp.sum(gnorms, axis=0)
    run_b.take(come)
    finish([run_a, run_b, run_c, run_d])
    s_a, s_b, s_c, s_down = (run.done for run in (run_a, run_b, run_c, run_d))
    merge = lambda a, b: jnp.concatenate([a, b], axis=1)
    return (
        layer_out,
        gtok,
        gnorms[0],
        s_c[0],
        s_c[1, :, :latw],
        s_c[1, :up_rows, latw : latw + up_width],
        s_c[1, up_rows:, latw : latw + up_width],
        merge(s_b[0, :, :lead], s_b[1, :, :lead]),
        gnorms[1],
        merge(s_a[0], s_b[0, :, lead:]),
        merge(s_a[1], s_b[1, :, lead:]),
        merge(s_down[0], s_down[1]),
    )


def solution(mesh):
    split = ("dp", "fsdp")
    flat, matrix = P(split), P(split, None)
    return jax.shard_map(
        shards,
        mesh=mesh,
        in_specs=(
            matrix,
            matrix,
            flat,
            matrix,
            matrix,
            matrix,
            matrix,
            matrix,
            flat,
            matrix,
            matrix,
            matrix,
            matrix,
        ),
        out_specs=(
            matrix,
            matrix,
            flat,
            matrix,
            matrix,
            matrix,
            matrix,
            matrix,
            flat,
            matrix,
            matrix,
            matrix,
        ),
        check_vma=False,
    )
```

```python
import functools

import jax
import jax.numpy as jnp
from jax import lax
from jax.experimental import pallas as pl
from jax.experimental.pallas import tpu as pltpu
from jax.sharding import PartitionSpec as P

HD = 64
G = 2
HG = 8
PAIR = 128
EPSILON = 1e-05
SCORE_SCALE = 0.125
NEGATIVE = -1e30
LOG2E = 1.4426950408889634
F32 = jnp.float32
BF16 = jnp.bfloat16
TILE = 256
QT = 128
SPAN = 4
PP = 2
PPB = 2
VMEM_LIMIT = 60 * 1024 * 1024


def nn(a, b):
    return lax.dot_general(a, b, (((1,), (0,)), ((), ())), preferred_element_type=F32)


def nt(a, b):
    return lax.dot_general(a, b, (((1,), (1,)), ((), ())), preferred_element_type=F32)


def tn(a, b):
    return lax.dot_general(a, b, (((0,), (0,)), ((), ())), preferred_element_type=F32)


def params(**extra):
    return pltpu.CompilerParams(vmem_limit_bytes=VMEM_LIMIT, **extra)


def whole(shape):
    return pl.BlockSpec(shape, lambda *_: (0,) * len(shape))


def rows_of(tile, width):
    return pl.BlockSpec((tile, width), lambda i: (i, 0))


def cost(micros):
    return pl.CostEstimate(flops=int(micros * 1.1e9), bytes_accessed=0, transcendentals=0)


def shape_of(shape, dtype):
    return jax.ShapeDtypeStruct(shape, dtype)


def project_kernel(
    tok_ref,
    wq_ref,
    wl_ref,
    wg_ref,
    ku_ref,
    vu_ref,
    q_ref,
    lat_ref,
    latt_ref,
    k_ref,
    v_ref,
    nt_ref,
    gain_ref,
):
    @pl.when(pl.program_id(0) == 0)
    def _():
        gain_ref[...] = wg_ref[...].astype(F32).T[0:8, :]

    x = tok_ref[...].astype(F32)
    root = lax.rsqrt(jnp.mean(x * x, axis=-1, keepdims=True) + EPSILON)
    normed = (x * root * gain_ref[0:1, :]).astype(BF16)
    nt_ref[...] = normed.T
    lat = nn(normed, wl_ref[...]).astype(BF16)
    lat_ref[...] = lat
    latt_ref[...] = lat.T
    q_ref[...] = (nn(normed, wq_ref[...]).astype(BF16).astype(F32) * SCORE_SCALE).astype(BF16)
    wide = lat.shape[1] // G
    out = k_ref.shape[1] // G
    for g in range(G):
        piece = lat[:, g * wide : (g + 1) * wide]
        k_ref[:, g * out : (g + 1) * out] = nn(
            piece, ku_ref[g * wide : (g + 1) * wide, :]
        ).astype(BF16)
        v_ref[:, g * out : (g + 1) * out] = nn(
            piece, vu_ref[g * wide : (g + 1) * wide, :]
        ).astype(BF16)


def columns_of(height, tile):
    return pl.BlockSpec((height, tile), lambda i: (0, i))


def project(tokens, first, ku, vu):
    count, d = tokens.shape
    latw = ku.shape[0]
    width = G * ku.shape[1]
    return pl.pallas_call(
        project_kernel,
        grid=(count // TILE,),
        in_specs=[
            rows_of(TILE, d),
            pl.BlockSpec((d, width), lambda i: (0, 0)),
            pl.BlockSpec((d, latw), lambda i: (0, width // latw)),
            pl.BlockSpec((d, PAIR), lambda i: (0, (d + ku.shape[1]) // PAIR)),
            whole(ku.shape),
            whole(vu.shape),
        ],
        out_specs=[
            rows_of(TILE, width),
            rows_of(TILE, latw),
            columns_of(latw, TILE),
            rows_of(TILE, width),
            rows_of(TILE, width),
            columns_of(d, TILE),
            whole((8, d)),
        ],
        out_shape=[
            shape_of((count, width), BF16),
            shape_of((count, latw), BF16),
            shape_of((latw, count), BF16),
            shape_of((count, width), BF16),
            shape_of((count, width), BF16),
            shape_of((d, count), BF16),
            shape_of((8, d), F32),
        ],
        cost_estimate=cost(10),
        compiler_params=params(),
        name="project",
    )(tokens, first[0], first[0], first[1], ku, vu)


def visible(doc):
    length = doc.shape[1]
    ids = doc.reshape(length)
    blocks = []
    padded = jnp.concatenate([jnp.full((SPAN * QT,), -1, ids.dtype), ids])
    for b in range(length // QT):
        keys = jnp.arange((b - SPAN) * QT, (b + 1) * QT)
        own = ids[b * QT : (b + 1) * QT]
        theirs = padded[b * QT : (b + SPAN + 1) * QT]
        queries = jnp.arange(b * QT, (b + 1) * QT)
        seen = (theirs[:, None] == own[None, :]) & (keys[:, None] <= queries[None, :])
        blocks.append(jnp.where(seen, 0.0, NEGATIVE))
    return jnp.stack(blocks).astype(BF16)


def split_heads(values):
    low = lax.broadcasted_iota(jnp.int32, values.shape, 1) < HD
    zero = jnp.zeros_like(values)
    return jnp.concatenate([jnp.where(low, values, zero), jnp.where(low, zero, values)], axis=0)


def attend_kernel(q_ref, k_ref, v_ref, mask_ref, o_ref, ot_ref, lse_ref):
    length = q_ref.shape[0]
    low = lax.broadcasted_iota(jnp.int32, (QT, PAIR), 1) < HD
    for b in range(length // QT):
        rows = slice(b * QT, (b + 1) * QT)
        extra = min(b, SPAN)
        keys = slice((b - extra) * QT, (b + 1) * QT)
        bias = mask_ref[b, (SPAN - extra) * QT :, :].astype(F32)
        bias = jnp.concatenate([bias, bias], axis=1)
        for pair in range(PP):
            cols = slice(pair * PAIR, (pair + 1) * PAIR)
            s = nt(k_ref[keys, cols], split_heads(q_ref[rows, cols])) * LOG2E + bias
            top = jnp.max(s, axis=0, keepdims=True)
            p = jnp.exp2(s - top).astype(BF16)
            v = v_ref[keys, cols]
            r = tn(p, jnp.concatenate([v, jnp.ones_like(v)], axis=1))
            r = jnp.where(
                jnp.concatenate([low, low], axis=1), r[:QT], r[QT:]
            )
            o = r[:, :PAIR] / r[:, PAIR:]
            o_ref[rows, cols] = o.astype(BF16)
            ot_ref[cols, rows] = o.T.astype(BF16)
            total = jnp.log2(r[:, PAIR:].T)
            lse_ref[pair, 0:1, rows] = top[:, :QT] + total[0:1]
            lse_ref[pair, 1:2, rows] = top[:, QT:] + total[HD : HD + 1]


def attend(mask, q, k, v, start, pairs):
    length = q.shape[0]
    width = pairs * PAIR
    wide = PP * PAIR
    strip = pl.BlockSpec((length, wide), lambda i: (0, start // PP + i))
    return pl.pallas_call(
        attend_kernel,
        grid_spec=pltpu.PrefetchScalarGridSpec(
            num_scalar_prefetch=0,
            grid=(pairs // PP,),
            in_specs=[strip, strip, strip, whole(mask.shape)],
            out_specs=[
                pl.BlockSpec((length, wide), lambda i: (0, i)),
                pl.BlockSpec((wide, length), lambda i: (i, 0)),
                pl.BlockSpec((PP, 8, length), lambda i: (i, 0, 0)),
            ],
        ),
        out_shape=[
            shape_of((length, width), BF16),
            shape_of((width, length), BF16),
            shape_of((pairs, 8, length), F32),
        ],
        cost_estimate=cost(2.5 * pairs),
        compiler_params=params(),
        name="attend",
    )(q, k, v, mask)


def attend_back_kernel(
    q_ref,
    k_ref,
    v_ref,
    o_ref,
    do_ref,
    lse_ref,
    mask_ref,
    dq_ref,
    dk_ref,
    dv_ref,
    dk_acc,
    dv_acc,
):
    length = q_ref.shape[0]
    low = lax.broadcasted_iota(jnp.int32, (QT, PAIR), 1) < HD
    dk_acc[...] = jnp.zeros_like(dk_acc)
    dv_acc[...] = jnp.zeros_like(dv_acc)
    kts = [k_ref[:, pair * PAIR : (pair + 1) * PAIR].T for pair in range(PPB)]
    for b in range(length // QT):
        rows = slice(b * QT, (b + 1) * QT)
        extra = min(b, SPAN)
        keys = slice((b - extra) * QT, (b + 1) * QT)
        bias = mask_ref[b, (SPAN - extra) * QT :, :].astype(F32)
        bias = jnp.concatenate([bias, bias], axis=1)
        for pair in range(PPB):
            cols = slice(pair * PAIR, (pair + 1) * PAIR)
            do = do_ref[rows, cols]
            prod = (do.astype(F32) * o_ref[rows, cols].astype(F32)).T
            inner = jnp.concatenate(
                [
                    jnp.sum(prod[:HD], axis=0, keepdims=True),
                    jnp.sum(prod[HD:], axis=0, keepdims=True),
                ],
                axis=1,
            )
            lse = jnp.concatenate(
                [lse_ref[pair, 0:1, rows], lse_ref[pair, 1:2, rows]], axis=1
            )
            qs = split_heads(q_ref[rows, cols])
            dos = split_heads(do)
            k = k_ref[keys, cols]
            p = jnp.exp2(nt(k, qs) * LOG2E + bias - lse)
            ds = (p * (nt(v_ref[keys, cols], dos) - inner)).astype(BF16)
            dv_acc[keys, cols] += nn(p.astype(BF16), dos)
            dk_acc[keys, cols] += nn(ds, qs)
            dq = nn(kts[pair][:, keys], ds) * SCORE_SCALE
            dq = jnp.concatenate([dq[:HD, :QT], dq[HD:, QT:]], axis=0)
            dq_ref[rows, cols] = dq.T.astype(BF16)
    dk_ref[...] = dk_acc[...].astype(BF16)
    dv_ref[...] = dv_acc[...].astype(BF16)


def attend_back(mask, q, k, v, o, do, lse, start, at, pairs):
    length = q.shape[0]
    width = pairs * PAIR
    wide = PPB * PAIR
    strip = pl.BlockSpec((length, wide), lambda i: (0, start // PPB + i))
    own = pl.BlockSpec((length, wide), lambda i: (0, i))
    return pl.pallas_call(
        attend_back_kernel,
        grid_spec=pltpu.PrefetchScalarGridSpec(
            num_scalar_prefetch=0,
            grid=(pairs // PPB,),
            in_specs=[
                strip,
                strip,
                strip,
                pl.BlockSpec((length, wide), lambda i: (0, at // PPB + i)),
                strip,
                pl.BlockSpec((PPB, 8, length), lambda i: (at // PPB + i, 0, 0)),
                whole(mask.shape),
            ],
            out_specs=[own] * 3,
            scratch_shapes=[
                pltpu.VMEM((length, wide), F32),
                pltpu.VMEM((length, wide), F32),
            ],
        ),
        out_shape=[shape_of((length, width), BF16)] * 3,
        cost_estimate=cost(3.5 * pairs),
        compiler_params=params(),
        name="attend_back",
    )(q, k, v, o, do, lse, mask)


def middle_kernel(*refs):
    att_refs = refs[:-6]
    wo_ref, tok_ref, gain_ref, hid_ref, mid_ref, midt_ref = refs[-6:]
    att = jnp.concatenate([ref[...] for ref in att_refs], axis=1)
    hid = tok_ref[...].astype(F32) + nn(att, wo_ref[...])
    hid_ref[...] = hid
    root = lax.rsqrt(jnp.mean(hid * hid, axis=-1, keepdims=True) + EPSILON)
    mid = (hid * root * gain_ref[1:2, :]).astype(BF16)
    mid_ref[...] = mid
    midt_ref[...] = mid.T


def middle(att, wo, tokens, gains):
    count, d = tokens.shape
    return pl.pallas_call(
        middle_kernel,
        grid=(count // TILE,),
        in_specs=[rows_of(TILE, x.shape[1]) for x in att]
        + [wo[1], rows_of(TILE, d), whole((8, d))],
        out_specs=[rows_of(TILE, d), rows_of(TILE, d), columns_of(d, TILE)],
        out_shape=[
            shape_of((count, d), F32),
            shape_of((count, d), BF16),
            shape_of((d, count), BF16),
        ],
        cost_estimate=cost(8),
        compiler_params=params(),
        name="middle",
    )(*att, wo[0], tokens, gains)


def unfold_kernel(own_rows, down_rows, in_ref, out_ref):
    d = out_ref.shape[1]
    for device in range(in_ref.shape[0] // own_rows):
        for fold in range(in_ref.shape[1] // d):
            count = min(own_rows, down_rows - fold * own_rows)
            at = device * down_rows + fold * own_rows
            out_ref[at : at + count, :] = in_ref[
                device * own_rows : device * own_rows + count, fold * d : (fold + 1) * d
            ]


def unfold(wide, own_rows, down_rows, d):
    folds = -(-down_rows // own_rows)
    devices = wide.shape[0] // own_rows
    if own_rows % 16 or devices % 8:
        down = wide[:, : folds * d].reshape(devices, own_rows, folds, d).transpose(0, 2, 1, 3)
        down = down.reshape(devices, folds * own_rows, d)[:, :down_rows]
        return down.reshape(devices * down_rows, d)
    return pl.pallas_call(
        functools.partial(unfold_kernel, own_rows, down_rows),
        grid=(devices // 8,),
        in_specs=[pl.BlockSpec((8 * own_rows, folds * d), lambda i: (i, 0))],
        out_specs=pl.BlockSpec((8 * down_rows, d), lambda i: (i, 0)),
        out_shape=shape_of((devices * down_rows, d), BF16),
        cost_estimate=cost(5),
        compiler_params=params(),
        name="unfold",
    )(wide)


def owner_rows(core_ref, pair, height, mine, span=None):
    core = core_ref[0]
    first = 2 * pair if span is None else 2 * pair % span
    which = first + (core if mine else 1 - core)
    return pl.ds(pl.multiple_of(which * height, height), height)


def feed_kernel(first, core_ref, *refs):
    refs = list(refs)
    mid_ref, midt_ref, cot_ref = refs[:3]
    del refs[:3]
    gfrom_ref = None
    if not first:
        gfrom_ref = refs[0]
        del refs[:2]
    gate_ref, up_ref, down_ref, gmid_ref, act_ref, keep_ref, send_ref, gdown_ref = refs[:8]
    gmid_acc, act_s, ggp_s, gup_s, gp_s, up_s, ga_s = refs[8:]

    @pl.when(pl.program_id(0) == 0)
    def _():
        if first:
            gmid_acc[...] = jnp.zeros_like(gmid_acc)
        else:
            gmid_acc[...] = gfrom_ref[...]

    gate = gate_ref[...]
    up = up_ref[...]

    slot = pl.program_id(0) % 2
    steps = pl.num_programs(0) - 1
    _, pairs, height, _ = keep_ref.shape
    half = cot_ref.shape[1] // 2

    count = mid_ref.shape[0]
    tile = count // 4

    def products():
        m = mid_ref[...]
        gp_s[...] = nn(m, gate)
        up_s[...] = nn(m, up)
        ga_s[...] = nt(cot_ref[...], down_ref[...])

    def pointwise(r):
        rows = slice(r * tile, (r + 1) * tile)
        gate_pre, up_pre, grad_act = gp_s[rows, :], up_s[rows, :], ga_s[rows, :]
        sig = 0.5 * jnp.tanh(0.5 * gate_pre) + 0.5
        silu = gate_pre * sig
        act = (silu * up_pre).astype(BF16)
        act_ref[rows, :] = act
        act_s[slot, rows, :] = act
        ggp_s[slot, rows, :] = (grad_act * up_pre * (sig + silu * (1.0 - sig))).astype(BF16)
        gup_s[slot, rows, :] = (grad_act * silu).astype(BF16)

    def sums():
        gmid_acc[...] += nt(ggp_s[slot], gate) + nt(gup_s[slot], up)

    def grads(r):
        ggp, gup, act = ggp_s[1 - slot], gup_s[1 - slot], act_s[1 - slot]
        mine, ref = ((False, send_ref), (True, keep_ref))[r % 2]
        if r < 2:
            rows = [midt_ref[owner_rows(core_ref, p, height, mine), :] for p in range(pairs)]
            m = jnp.concatenate(rows, axis=0)
            ref[0] = nn(m, ggp).astype(BF16).reshape(ref.shape[1:])
            ref[1] = nn(m, gup).astype(BF16).reshape(ref.shape[1:])
        else:
            cols = slice((r - 2) * half, (r - 1) * half)
            gdown_ref[r - 2] = tn(act, cot_ref[:, cols]).astype(BF16)

    def first_half():
        products()
        for r in range(4):
            pointwise(r)
        sums()

    def second_half():
        for r in range(4):
            grads(r)

    def both_halves():
        products()
        for r in range(4):
            grads(r)
            pointwise(r)
        sums()

    @pl.when(pl.program_id(0) == 0)
    def _():
        first_half()

    @pl.when((pl.program_id(0) > 0) & (pl.program_id(0) < steps))
    def _():
        both_halves()

    @pl.when(pl.program_id(0) == steps)
    def _():
        second_half()

    @pl.when(pl.program_id(0) == pl.num_programs(0) - 1)
    def _():
        gmid_ref[...] = gmid_acc[...]


def feed(core, mid, midt, cot, before, gate, up, down, span, lead, n_dp, ff):
    count, d = mid.shape
    first = before is None
    at, steps = span[0], span[1] - span[0]
    args = [mid, midt, cot]
    specs = [whole((count, d)), whole((d, count)), whole((count, d))]
    alias = {}
    if not first:
        args += list(before)
        specs += [whole((count, d)), pl.BlockSpec(memory_space=pl.ANY)]
        alias = {5: 4}
    height = d // n_dp
    now = lambda i: jnp.minimum(i, steps - 1)
    past = lambda i: jnp.maximum(i - 1, 0)
    strip = pl.BlockSpec((2, n_dp // 2, height, TILE), lambda i, *_: (0, 0, 0, past(i) + lead // TILE))
    grads = shape_of((2, n_dp // 2, height, lead + steps * TILE), BF16)
    return pl.pallas_call(
        functools.partial(feed_kernel, first),
        grid_spec=pltpu.PrefetchScalarGridSpec(
            num_scalar_prefetch=1,
            grid=(steps + 1,),
            in_specs=specs
            + [
                pl.BlockSpec((d, TILE), lambda i, *_: (0, gate[1] + at + now(i))),
                pl.BlockSpec((d, TILE), lambda i, *_: (0, up[1] + at + now(i))),
                pl.BlockSpec((TILE, d), lambda i, *_: (at + now(i), 0)),
            ],
            out_specs=[
                whole((count, d)),
                pl.BlockSpec((count, TILE), lambda i, *_: (0, now(i))),
                strip,
                strip,
                pl.BlockSpec((2, TILE, d // 2), lambda i, *_: (0, at + past(i), 0)),
            ],
            scratch_shapes=[pltpu.VMEM((count, d), F32)]
            + [pltpu.VMEM((2, count, TILE), BF16)] * 3
            + [pltpu.VMEM((count, TILE), F32)] * 3,
        ),
        out_shape=[
            shape_of((count, d), F32),
            shape_of((count, steps * TILE), BF16),
            grads,
            grads,
            shape_of((2, ff, d // 2), BF16),
        ],
        input_output_aliases=alias,
        cost_estimate=cost(5.5 * steps),
        compiler_params=params(),
        name="feed",
    )(core, *args, gate[0], up[0], down)


def leave_kernel(hid_ref, *refs):
    act_refs, down_ref, out_ref = refs[:-2], refs[-2], refs[-1]
    total = hid_ref[...]
    at = 0
    for ref in act_refs:
        wide = ref.shape[1]
        total += nn(ref[...], down_ref[at : at + wide, :])
        at += wide
    out_ref[...] = total.astype(BF16)


def leave(hid, acts, down):
    count, d = hid.shape
    tile = 2 * TILE
    return pl.pallas_call(
        leave_kernel,
        grid=(count // tile,),
        in_specs=[rows_of(tile, d)] + [rows_of(tile, x.shape[1]) for x in acts] + [whole(down.shape)],
        out_specs=rows_of(tile, d),
        out_shape=shape_of((count, d), BF16),
        cost_estimate=cost(9),
        compiler_params=params(),
        name="leave",
    )(hid, *acts, down)


def middle_back_kernel(
    core_ref,
    gmid_ref,
    hid_ref,
    cot_ref,
    *refs,
):
    attt_refs = refs[:-10]
    (
        wo_ref,
        gain_ref,
        keep_in,
        send_in,
        ghid_ref,
        gatt_ref,
        keep_ref,
        send_ref,
        gn_ref,
        branch_s,
    ) = refs[-10:]
    step = pl.program_id(0)
    tile = hid_ref.shape[0]

    @pl.when(step == 0)
    def _():
        gn_ref[...] = jnp.zeros_like(gn_ref)

    hid = hid_ref[...]
    root = lax.rsqrt(jnp.mean(hid * hid, axis=-1, keepdims=True) + EPSILON)
    unit = hid * root
    gmid = gmid_ref[...]
    gn_ref[0:1, :] += jnp.sum(gmid * unit, axis=0, keepdims=True)
    t = gmid * gain_ref[1:2, :]
    inner = jnp.mean(t * unit, axis=-1, keepdims=True)
    ghid = cot_ref[...].astype(F32) + root * (t - unit * inner)
    ghid_ref[...] = ghid
    branch = ghid.astype(BF16)
    gatt_ref[...] = nt(branch, wo_ref[...]).astype(BF16)
    branch_s[pl.ds(pl.multiple_of(step * tile, tile), tile), :] = branch

    @pl.when(step == pl.num_programs(0) - 1)
    def _():
        half = branch_s.shape[1] // 2
        _, pairs, height, _ = keep_ref.shape
        tall = attt_refs[0].shape[0]
        for p in range(pairs):
            for mine, ref in ((False, send_ref), (True, keep_ref)):
                attt_ref = attt_refs[2 * p * height // tall]
                rows = attt_ref[owner_rows(core_ref, p, height, mine, tall // height), :]
                grad = nn(rows, branch_s[...]).astype(BF16)
                ref[0, p] = grad[:, :half]
                ref[1, p] = grad[:, half:]


def middle_back(core, gmid, hid, cot, attt, wo, gains, keep, send):
    count, d = hid.shape
    width = sum(x.shape[0] for x in attt)
    pairs, height = keep.shape[1:3]
    anywhere = pl.BlockSpec(memory_space=pl.ANY)
    strip = pl.BlockSpec((2, pairs, height, d // 2), lambda i, *_: (0, 0, 0, 0))
    tile = lambda wide: pl.BlockSpec((TILE, wide), lambda i, *_: (i, 0))
    return pl.pallas_call(
        middle_back_kernel,
        grid_spec=pltpu.PrefetchScalarGridSpec(
            num_scalar_prefetch=1,
            grid=(count // TILE,),
            in_specs=[
                tile(d),
                tile(d),
                tile(d),
            ]
            + [whole(x.shape) for x in attt]
            + [
                wo[1],
                whole((8, d)),
                anywhere,
                anywhere,
            ],
            out_specs=[tile(d), tile(width), strip, strip, whole((8, d))],
            scratch_shapes=[pltpu.VMEM((count, d), BF16)],
        ),
        out_shape=[
            shape_of((count, d), F32),
            shape_of((count, width), BF16),
            shape_of(keep.shape, BF16),
            shape_of(send.shape, BF16),
            shape_of((8, d), F32),
        ],
        input_output_aliases={6 + len(attt): 2, 7 + len(attt): 3},
        cost_estimate=cost(12),
        compiler_params=params(),
        name="middle_back",
    )(core, gmid, hid, cot, *attt, wo[0], gains, keep, send)


def interleave(up_rows, height):
    to = lax.broadcasted_iota(jnp.int32, (height, height), 0)
    start = lax.broadcasted_iota(jnp.int32, (height, height), 1)
    turn, row = to // (2 * up_rows), to % (2 * up_rows)
    late = (row >= up_rows).astype(jnp.int32)
    want = turn * up_rows + row - late * up_rows + late * (height // 2)
    return (start == want).astype(F32).astype(BF16)


def weights_back_kernel(up_rows, core_ref, *refs):
    parts = (len(refs) - 9) // 3
    gq_refs, gk_refs, gv_refs = refs[:parts], refs[parts : 2 * parts], refs[2 * parts : 3 * parts]
    latt_ref, nt_ref, ku_ref, vu_ref, glat_ref, keep_ref, send_ref, gku_s, gvu_s = refs[3 * parts :]
    wide = ku_ref.shape[0] // G
    out = ku_ref.shape[1]
    glats = [None] * G
    at = 0
    for part in range(parts):
        strip = gk_refs[part].shape[1]
        g, start = at // out, at % out
        own, cols = slice(g * wide, (g + 1) * wide), slice(start, start + strip)
        gk, gv = gk_refs[part][...], gv_refs[part][...]
        here = nt(gk, ku_ref[own, cols]) + nt(gv, vu_ref[own, cols])
        glats[g] = here if glats[g] is None else glats[g] + here
        gku_s[own, cols] = nn(latt_ref[own, :], gk)
        gvu_s[own, cols] = nn(latt_ref[own, :], gv)
        at += strip
    for g in range(G):
        glat_ref[:, g * wide : (g + 1) * wide] = glats[g].astype(BF16)
    _, pairs, height, _ = keep_ref.shape
    latw = glat_ref.shape[1]
    owners = height // (2 * up_rows)
    core = core_ref[0]
    for mine, ref in ((False, send_ref), (True, keep_ref)):
        rows = [nt_ref[owner_rows(core_ref, p, height, mine), :] for p in range(pairs)]
        m = jnp.concatenate(rows, axis=0)
        at = 0
        for gq_ref in gq_refs:
            strip = gq_ref.shape[1]
            grad = nn(m, gq_ref[...]).astype(BF16)
            ref[0, :, :, at : at + strip] = grad.reshape(pairs, height, strip)
            at += strip
        grad = nn(m, glat_ref[...]).astype(BF16)
        ref[1, :, :, 0:latw] = grad.reshape(pairs, height, latw)
        for p in range(pairs):
            which = 2 * p + (core if mine else 1 - core)
            near = pl.ds(pl.multiple_of(which * (height // 2), height // 2), height // 2)
            keys, values = gku_s[near, :], gvu_s[near, :]
            if up_rows % 8:
                both = jnp.concatenate([keys, values], axis=0).astype(BF16)
                ups = nn(interleave(up_rows, height), both)
            else:
                pieces = []
                for j in range(owners):
                    pieces.append(keys[j * up_rows : (j + 1) * up_rows])
                    pieces.append(values[j * up_rows : (j + 1) * up_rows])
                ups = jnp.concatenate(pieces, axis=0)
            ref[1, p, :, latw : latw + out] = ups.astype(BF16)


def weights_back(core, gq, gk, gv, latt, nt_, ku, vu, n_dp, up_rows):
    count = gq[0].shape[0]
    d = nt_.shape[0]
    width = sum(x.shape[1] for x in gq)
    latw = latt.shape[0]
    grads = (2, n_dp // 2, d // n_dp, width)
    args = [*gq, *gk, *gv, latt, nt_, ku, vu]
    return pl.pallas_call(
        functools.partial(weights_back_kernel, up_rows),
        grid_spec=pltpu.PrefetchScalarGridSpec(
            num_scalar_prefetch=1,
            grid=(1,),
            in_specs=[whole(x.shape) for x in args],
            out_specs=[whole((count, latw)), whole(grads), whole(grads)],
            scratch_shapes=[pltpu.VMEM(ku.shape, F32), pltpu.VMEM(vu.shape, F32)],
        ),
        out_shape=[shape_of((count, latw), BF16), shape_of(grads, BF16), shape_of(grads, BF16)],
        cost_estimate=cost(11),
        compiler_params=params(),
        name="weights_back",
    )(core, *args)


def tokens_back_kernel(*refs):
    glat_ref, tok_ref, ghid_ref, wq_ref, wl_ref, gain_ref, gtok_ref, gn_ref = refs[-8:]
    gq_refs = refs[:-8]

    @pl.when(pl.program_id(0) == 0)
    def _():
        gn_ref[...] = jnp.zeros_like(gn_ref)

    gq = jnp.concatenate([ref[...] for ref in gq_refs], axis=1)
    gin = nt(gq, wq_ref[...]) + nt(glat_ref[...], wl_ref[...])
    x = tok_ref[...].astype(F32)
    root = lax.rsqrt(jnp.mean(x * x, axis=-1, keepdims=True) + EPSILON)
    unit = x * root
    gn_ref[0:1, :] += jnp.sum(gin * unit, axis=0, keepdims=True)
    t = gin * gain_ref[0:1, :]
    inner = jnp.mean(t * unit, axis=-1, keepdims=True)
    gtok_ref[...] = (ghid_ref[...] + root * (t - unit * inner)).astype(BF16)


def tokens_back(gq, glat, tokens, ghid, first, gains):
    count, d = tokens.shape
    width = sum(x.shape[1] for x in gq)
    latw = glat.shape[1]
    return pl.pallas_call(
        tokens_back_kernel,
        grid=(count // TILE,),
        in_specs=[rows_of(TILE, x.shape[1]) for x in gq]
        + [
            rows_of(TILE, latw),
            rows_of(TILE, d),
            rows_of(TILE, d),
            pl.BlockSpec((d, width), lambda i: (0, 0)),
            pl.BlockSpec((d, latw), lambda i: (0, width // latw)),
            whole((8, d)),
        ],
        out_specs=[rows_of(TILE, d), whole((8, d))],
        out_shape=[shape_of((count, d), BF16), shape_of((8, d), F32)],
        cost_estimate=cost(8),
        compiler_params=params(),
        name="tokens_back",
    )(*gq, glat, tokens, ghid, first[0], first[0], gains)


def swap(values, axis_name, bit):
    size = lax.axis_size(axis_name)
    return lax.ppermute(values, axis_name, [(i, i ^ bit) for i in range(size)])


def bits_of(axis_name):
    size = lax.axis_size(axis_name)
    return [1 << i for i in range(size.bit_length() - 1)]


def owner_bits():
    names = [("dp", bit) for bit in reversed(bits_of("dp")) if bit > 1]
    return names + [("fsdp", bit) for bit in reversed(bits_of("fsdp"))]


def add(a, b, dtype=BF16):
    return (a.astype(F32) + b.astype(F32)).astype(dtype)


def part_of(values, names, which, mine, trail=2):
    axis_name, bit = which
    own = (lax.axis_index(axis_name) // bit) % 2
    at = values.ndim - trail - len(names) + names.index(which)
    return lax.dynamic_index_in_dim(values, own if mine else 1 - own, at, keepdims=False)


def scatter_rounds(keep, send):
    (came,) = yield [(send, "dp", 1)]
    names = owner_bits()
    rows = keep.size // (2 * keep.shape[-1]) >> len(names)
    shape = (2,) * len(names) + (rows, keep.shape[-1])
    keep, came = keep.reshape((2,) + shape), came.reshape((2,) + shape)
    firsts = [("fsdp", 1), ("dp", 2)]
    parts = [(keep[0], came[0]), (keep[1], came[1])]
    left = [names, names]
    for orders in (firsts, firsts[::-1]):
        split = [
            [add(*(part_of(x, kept, which, mine) for x in part)) for mine in (False, True)]
            for part, kept, which in zip(parts, left, orders)
        ]
        come = yield [(send, *which) for (send, _), which in zip(split, orders)]
        parts = [(keep, here) for (_, keep), here in zip(split, come)]
        left = [
            [name for name in kept if name != which] for kept, which in zip(left, orders)
        ]
    both, names = jnp.stack([add(*part) for part in parts]), left[0]
    rest = sorted(names, key=lambda name: (name[0] != "fsdp", name[1]))
    for which in rest:
        (came,) = yield [(part_of(both, names, which, False), *which)]
        both = add(
            part_of(both, names, which, True), came, F32 if which == rest[-1] else BF16
        )
        names = [name for name in names if name != which]
    return both


def gather_rounds(values):
    names = owner_bits()
    firsts = [("fsdp", 1), ("dp", 2)]
    rest = [name for name in names if name not in firsts]
    rest = sorted(rest, key=lambda name: (name[0] != "fsdp", name[1]), reverse=True)
    every = [("dp", 1 << i) for i in reversed(range(len(bits_of("dp"))))]
    every += [("fsdp", 1 << i) for i in reversed(range(len(bits_of("fsdp"))))]

    def join(part, came, have, which):
        have = sorted(have + [which], key=every.index)
        axis_name, bit = which
        low = (lax.axis_index(axis_name) // bit) % 2 == 0
        pair = (jnp.where(low, part, came), jnp.where(low, came, part))
        return jnp.stack(pair, axis=have.index(which)), have

    have = []
    for which in rest:
        (came,) = yield [(values, *which)]
        values, have = join(values, came, have, which)
    cut = values.shape[-1] // 256 * 128
    parts = [values[..., :cut], values[..., cut:]]
    haves = [have, have]
    for orders in (firsts, firsts[::-1], [("dp", 1)] * 2):
        come = yield [(part, *which) for part, which in zip(parts, orders)]
        both = [join(*item) for item in zip(parts, come, haves, orders)]
        parts, haves = [x[0] for x in both], [x[1] for x in both]
    return [part.reshape(-1, part.shape[-1]) for part in parts]


class Rounds:
    def __init__(self, steps):
        self.steps = steps
        self.wants = next(self.steps)
        self.done = None

    def after(self, other):
        values = [want[0] for want in self.wants]
        values, _ = lax.optimization_barrier((values, [want[0] for want in other.wants]))
        self.wants = [(value, *want[1:]) for value, want in zip(values, self.wants)]

    def take(self, come):
        try:
            self.wants = self.steps.send(come)
        except StopIteration as end:
            self.wants, self.done = [], end.value


def beside(held, runs, work):
    sends = [[want[0] for want in run.wants] for run in runs]
    held, sends = lax.optimization_barrier((held, sends))
    come = [
        [swap(values, *want[1:]) for values, want in zip(group, run.wants)]
        for group, run in zip(sends, runs)
    ]
    result = work(held)
    result, come = lax.optimization_barrier((result, come))
    for run, here in zip(runs, come):
        run.take(here)
    return result


def together(runs):
    beside((), runs, lambda held: held)


def finish(runs):
    while any(run.wants for run in runs):
        live = [run for run in runs if run.wants]
        come = [[swap(*want) for want in run.wants] for run in live]
        for run, here in zip(live, come):
            run.take(here)


def shards(
    tokens,
    doc_ids,
    norm_in,
    query_weight,
    latent_weight,
    key_up_weight,
    value_up_weight,
    output_weight,
    norm_mid,
    gate_weight,
    up_weight,
    down_weight,
    cotangent,
):
    both = ("dp", "fsdp")
    n_dp = lax.axis_size("dp")
    devices = n_dp * lax.axis_size("fsdp")
    own_rows, d = query_weight.shape
    d_all = own_rows * devices
    latw = latent_weight.shape[1]
    up_rows, up_width = key_up_weight.shape
    ff = gate_weight.shape[1]

    gains = jnp.stack([norm_in, norm_mid], axis=1)
    gains = jnp.pad(gains, ((0, 0), (0, PAIR - 2)))
    packed = jnp.concatenate(
        [
            query_weight,
            latent_weight,
            output_weight,
            jnp.concatenate([key_up_weight, value_up_weight], axis=0),
            gains,
        ],
        axis=1,
    )
    steps = ff // TILE
    cut = -(-steps * 5 // 8)
    (gate_weight, up_weight, down_weight), packed = lax.optimization_barrier(
        ((gate_weight, up_weight, down_weight), packed)
    )
    down_rows = down_weight.shape[0]
    folds = -(-down_rows // own_rows)
    down_own = jnp.pad(down_weight, ((0, folds * own_rows - down_rows), (0, 0)))
    middle_at = cut * TILE
    wide = [
        jnp.concatenate(
            [down_own[i * own_rows : (i + 1) * own_rows] for i in range(folds)]
            + [gate_weight[:, :middle_at], up_weight[:, :middle_at]],
            axis=1,
        ),
        jnp.concatenate([gate_weight[:, middle_at:], up_weight[:, middle_at:]], axis=1),
    ]
    gate_at = folds * d // TILE
    get_first = Rounds(gather_rounds(packed))
    for _ in range(0):
        together([get_first])
    wide[0] = lax.all_gather(wide[0], both, axis=0, tiled=True)
    together([get_first])
    wide[1], _ = lax.optimization_barrier((wide[1], get_first.wants[0][0]))
    wide[1] = lax.all_gather(wide[1], both, axis=0, tiled=True)
    while get_first.wants:
        together([get_first])
    first = get_first.done

    ups = first[1][:, d : d + up_width].reshape(devices, 2, up_rows, up_width)
    ku = ups[:, 0].reshape(devices * up_rows, up_width)
    vu = ups[:, 1].reshape(devices * up_rows, up_width)
    mask = visible(doc_ids)
    core = (lax.axis_index("dp") % 2).astype(jnp.int32).reshape(1)

    q, lat, latt, k, v, normed_t, gain_rows = project(tokens, first, ku, vu)
    pairs = q.shape[1] // PAIR
    halves = [attend(mask, q, k, v, 0, pairs)]
    wo = (first[1], pl.BlockSpec((d_all, d), lambda i, *_: (0, 0)))
    hid, mid, midt = middle([half[0] for half in halves], wo, tokens, gain_rows)
    down = unfold(wide[0], own_rows, down_rows, d)
    gmid, act_a, keep_a, send_a, gdown = feed(
        core,
        mid,
        midt,
        cotangent,
        None,
        (wide[0], gate_at),
        (wide[0], gate_at + cut),
        down,
        (0, cut),
        0,
        n_dp,
        ff,
    )
    lead = d // 2
    run_a = Rounds(scatter_rounds(keep_a, send_a))
    gmid, act_b, keep_b, send_b, gdown = beside(
        gmid,
        [run_a],
        lambda gmid: feed(
            core,
            mid,
            midt,
            cotangent,
            (gmid, gdown),
            (wide[1], -cut),
            (wide[1], steps - 2 * cut),
            down,
            (cut, steps),
            lead,
            n_dp,
            ff,
        ),
    )
    split = gdown.reshape(2, n_dp // 2, 2, ff // n_dp, d // 2)
    run_d = Rounds(
        scatter_rounds(
            lax.dynamic_index_in_dim(split, core[0], 2, keepdims=False),
            lax.dynamic_index_in_dim(split, 1 - core[0], 2, keepdims=False),
        )
    )
    ghid, gatt, keep_b, send_b, gnorm_mid = beside(
        gmid,
        [run_a, run_d],
        lambda gmid: middle_back(
            core,
            gmid,
            hid,
            cotangent,
            [half[1] for half in halves],
            wo,
            gain_rows,
            keep_b,
            send_b,
        ),
    )
    run_b = Rounds(scatter_rounds(keep_b, send_b))
    gq, gk, gv = [], [], []
    half = halves[0]
    some = pairs // 4

    def attention_part(gatt, runs, start, count):
        pieces = beside(
            gatt,
            runs,
            lambda gatt: attend_back(
                mask, q, k, v, half[0], gatt, half[2], start, start, count
            ),
        )
        for kept, piece in zip((gq, gk, gv), pieces):
            kept.append(piece)

    attention_part(gatt, [run_a, run_b], 0, some)
    layer_out = beside(hid, [run_d, run_a], lambda hid: leave(hid, [act_a, act_b], down))
    attention_part(gatt, [run_d, run_a], some, some)
    attention_part(gatt, [run_b, run_d], 2 * some, pairs - 2 * some)
    glat, keep_c, send_c = beside(
        latt,
        [run_b, run_d],
        lambda latt: weights_back(
            core, gq, gk, gv, latt, normed_t, ku, vu, n_dp, up_rows
        ),
    )
    run_c = Rounds(scatter_rounds(keep_c, send_c))
    run_c.after(run_b)
    come = [swap(*want) for want in run_b.wants]
    together([run_c])
    come, _ = lax.optimization_barrier((come, [want[0] for want in run_c.wants]))
    run_b.take(come)
    come = [swap(*want) for want in run_b.wants]
    gtok, gnorm_in = beside(
        ghid, [run_c], lambda ghid: tokens_back(gq, glat, tokens, ghid, first, gain_rows)
    )
    kept, come = lax.optimization_barrier(([want[0] for want in run_c.wants], come))
    run_c.wants = [(value, *want[1:]) for value, want in zip(kept, run_c.wants)]
    gnorms = jnp.stack([gnorm_in[0], gnorm_mid[0]]).reshape(2, devices, own_rows)
    gnorms, _ = lax.optimization_barrier(
        (gnorms.transpose(1, 0, 2), [want[0] for want in run_c.wants])
    )
    gnorms = lax.all_to_all(gnorms, both, split_axis=0, concat_axis=0, tiled=True)
    together([run_c])
    while len(run_c.wants) > 0:
        gnorms = beside(gnorms, [run_c], lambda held: held)
    gnorms = jnp.sum(gnorms, axis=0)
    run_b.take(come)
    finish([run_a, run_b, run_c, run_d])
    s_a, s_b, s_c, s_down = (run.done for run in (run_a, run_b, run_c, run_d))
    merge = lambda a, b: jnp.concatenate([a, b], axis=1)
    return (
        layer_out,
        gtok,
        gnorms[0],
        s_c[0],
        s_c[1, :, :latw],
        s_c[1, :up_rows, latw : latw + up_width],
        s_c[1, up_rows:, latw : latw + up_width],
        merge(s_b[0, :, :lead], s_b[1, :, :lead]),
        gnorms[1],
        merge(s_a[0], s_b[0, :, lead:]),
        merge(s_a[1], s_b[1, :, lead:]),
        merge(s_down[0], s_down[1]),
    )


def solution(mesh):
    split = ("dp", "fsdp")
    flat, matrix = P(split), P(split, None)
    return jax.shard_map(
        shards,
        mesh=mesh,
        in_specs=(
            matrix,
            matrix,
            flat,
            matrix,
            matrix,
            matrix,
            matrix,
            matrix,
            flat,
            matrix,
            matrix,
            matrix,
            matrix,
        ),
        out_specs=(
            matrix,
            matrix,
            flat,
            matrix,
            matrix,
            matrix,
            matrix,
            matrix,
            flat,
            matrix,
            matrix,
            matrix,
        ),
        check_vma=False,
    )
```
